32 devices in a mesh: seqhi: 4 (over x, core), seqlo: 8 (over z, y).
Axes of the slice: x: 2, y: 2, z: 4, core: 2. Of those that a mesh axis runs over, the one named last changes fastest.
Arguments:
- queries: bfloat16 [8192, 2048], P(('seqhi', 'seqlo')), may hold values from -6 to 6
- keys: bfloat16 [8192, 128], P(('seqhi', 'seqlo')), may hold values from -6 to 6
- values: bfloat16 [8192, 128], P(('seqhi', 'seqlo')), may hold values from -6 to 6
- outputs: bfloat16 [8192, 2048], P(('seqhi', 'seqlo')), may hold values from -6 to 6
- out_grad: bfloat16 [8192, 2048], P(('seqhi', 'seqlo')), may hold values from -96 to 96
- lse: float32 [16, 8192], P(None, ('seqhi', 'seqlo')), may hold values from 7 to 9
- sink_keys: bfloat16 [128, 128], replicated, may hold values from -6 to 6
- sink_values: bfloat16 [128, 128], replicated, may hold values from -6 to 6
- window_len: int32 [16], replicated, may hold values from 256 to 2048, as said below
- sink_live: int32 [16], replicated, may hold values from 32 to 128, as said below
Outputs:
- query_grad: float32 [8192, 2048], P(('seqhi', 'seqlo'))
- key_grad: float32 [8192, 128], P(('seqhi', 'seqlo'))
- value_grad: float32 [8192, 128], P(('seqhi', 'seqlo'))
- sink_key_grad: float32 [128, 128], replicated
- sink_value_grad: float32 [128, 128], replicated
The draws below stay inside these ranges and needn't reach their ends.
Inputs may be any that keep to these rules, and one draw needn't show every extreme that they name: `window_len`: one head's window is exactly 2048. `sink_live`: one head reads all 128 initial keys.
All inputs are finite; a program needn't handle non-finite values.
Results may differ from the reference program's by a relative error of at most 0.0039.
Values may be sent and summed in bfloat16 or wider, within the bound.
No kernel may reach another device: no remote copies, remote signals or barrier semaphores. Data moves between devices by JAX's collectives and lax.ppermute only.
A program may use at most 64 MiB of HBM per device.

```python
import jax
import jax.numpy as jnp
from jax import lax

H = 16
DH = 128
WIN = 2048
SINK = 128
TOK_DEV = 256
TOKENS = 8192


def draw_window_len(key, part):
    key_spans, key_top = jax.random.split(jax.random.fold_in(key, 11))
    spans = jax.random.randint(key_spans, (H,), WIN // 8, WIN + 1, dtype=jnp.int32)
    chosen = jax.random.randint(key_top, (), 0, H, dtype=jnp.int32)
    return jnp.where(jnp.arange(H, dtype=jnp.int32) == chosen, WIN, spans).astype(jnp.int32)


def draw_sink_live(key, part):
    key_spans, key_top = jax.random.split(jax.random.fold_in(key, 23))
    spans = jax.random.randint(key_spans, (H,), SINK // 4, SINK + 1, dtype=jnp.int32)
    chosen = jax.random.randint(key_top, (), 0, H, dtype=jnp.int32)
    return jnp.where(jnp.arange(H, dtype=jnp.int32) == chosen, SINK, spans).astype(jnp.int32)


def level_of(stream_key, dims, shards, least, largest):
    level, own = 1.0, jax.random.fold_in(stream_key, 6)
    for axis_at, parts in shards:
        draws = jnp.exp(jax.random.uniform(jax.random.fold_in(own, axis_at), (parts,), jnp.float32, least / len(shards), largest / len(shards)))
        level = level * jnp.repeat(draws, dims[axis_at] // parts).reshape([-1 if axis == axis_at else 1 for axis in range(len(dims))])
    return level


def gaussian(key, shape, deviation, limit, cuts=(), kind=jnp.bfloat16):
    values = jax.random.normal(key, shape, jnp.float32) * deviation
    if len(cuts) > 0:
        values = level_of(key, shape, cuts, -0.22, 0.18) * values
    return jnp.clip(values, min=-limit, max=limit).astype(kind)


def setup_inputs(seed: int = 0) -> dict:
    seeds = jax.random.split(jax.random.key(seed), 11)
    queries = gaussian(seeds[0], (TOKENS, H * DH), 1.0, 6.0, ((0, 32),))
    keys = gaussian(seeds[1], (TOKENS, DH), 1.0, 6.0, ((0, 32),))
    values = gaussian(seeds[2], (TOKENS, DH), 1.0, 6.0, ((0, 32),))
    outputs = gaussian(seeds[3], (TOKENS, H * DH), 1.0, 6.0, ((0, 32),))
    out_grad = gaussian(seeds[4], (TOKENS, H * DH), 16.0, 96.0, ((0, 32),))
    lse = jnp.clip(7.0 + 2.0 * jax.random.uniform(seeds[5], (H, TOKENS), jnp.float32) ** level_of(seeds[5], (H, TOKENS), ((1, 32),), -0.2, 0.2), 7.0, 9.0)
    sink_keys = gaussian(seeds[6], (SINK, DH), 1.0, 6.0)
    sink_values = gaussian(seeds[7], (SINK, DH), 1.0, 6.0)
    window_len = draw_window_len(jax.random.fold_in(seeds[10], 71), 0)
    sink_live = draw_sink_live(jax.random.fold_in(seeds[10], 71), 0)
    return dict(queries=queries, keys=keys, values=values, outputs=outputs, out_grad=out_grad, lse=lse, sink_keys=sink_keys, sink_values=sink_values, window_len=window_len, sink_live=sink_live)


def low_round(array_value):
    return lax.optimization_barrier(array_value.astype(jnp.bfloat16)).astype(jnp.float32)


def reference(queries, keys, values, outputs, out_grad, lse, sink_keys, sink_values, window_len, sink_live):
    reach_count = WIN // TOK_DEV
    block_count = TOKENS // TOK_DEV
    key_count = (reach_count + 1) * TOK_DEV
    score_scale = DH ** -0.5
    joined = jnp.concatenate([keys, values], axis=1)
    padded = jnp.concatenate([jnp.zeros((reach_count * TOK_DEV, 2 * DH), jnp.bfloat16), joined], axis=0)
    sink_key_f = sink_keys.astype(jnp.float32)
    sink_value_f = sink_values.astype(jnp.float32)
    key_index = jnp.arange(key_count, dtype=jnp.int32)
    query_index = reach_count * TOK_DEV + jnp.arange(TOK_DEV, dtype=jnp.int32)
    distance_grid = query_index[:, None] - key_index[None, :]
    sink_index = jnp.arange(SINK, dtype=jnp.int32)

    def one_block(state_pair, block_id):
        grad_store, sink_grad = state_pair
        begin = (block_id * TOK_DEV).astype(jnp.int32)
        query_block = lax.dynamic_slice_in_dim(queries, begin, TOK_DEV, 0).reshape(TOK_DEV, H, DH).astype(jnp.float32)
        out_block = lax.dynamic_slice_in_dim(outputs, begin, TOK_DEV, 0).reshape(TOK_DEV, H, DH).astype(jnp.float32)
        grad_block = lax.dynamic_slice_in_dim(out_grad, begin, TOK_DEV, 0).reshape(TOK_DEV, H, DH).astype(jnp.float32)
        lse_block = lax.dynamic_slice_in_dim(lse, begin, TOK_DEV, 1)
        key_value = lax.dynamic_slice_in_dim(padded, begin, key_count, 0).astype(jnp.float32)
        key_part = key_value[:, :DH]
        value_part = key_value[:, DH:]
        first_valid = ((reach_count - block_id) * TOK_DEV).astype(jnp.int32)
        inside = (distance_grid >= 0)[None] & (distance_grid[None] < window_len[:, None, None]) & (key_index >= first_valid)[None, None, :]
        scores = jnp.einsum("thd,kd->htk", query_block, key_part) * score_scale
        probabilities = jnp.where(inside, jnp.exp(scores - lse_block[:, :, None]), 0.0)
        row_delta = jnp.einsum("thd,thd->ht", grad_block, out_block)
        dprobs = jnp.einsum("thd,kd->htk", grad_block, value_part)
        dscores = probabilities * (dprobs - row_delta[:, :, None])
        sink_inside = sink_index[None, None, :] < sink_live[:, None, None]
        sink_scores = jnp.einsum("thd,sd->hts", query_block, sink_key_f) * score_scale
        sink_probs = jnp.where(sink_inside, jnp.exp(sink_scores - lse_block[:, :, None]), 0.0)
        sink_dprobs = jnp.einsum("thd,sd->hts", grad_block, sink_value_f)
        sink_dscores = sink_probs * (sink_dprobs - row_delta[:, :, None])
        probs_low = low_round(probabilities)
        dscores_low = low_round(dscores)
        sink_probs_low = low_round(sink_probs)
        sink_ds_low = low_round(sink_dscores)
        query_grad = (jnp.einsum("htk,kd->thd", dscores_low, key_part) + jnp.einsum("hts,sd->thd", sink_ds_low, sink_key_f)) * score_scale
        key_grad = jnp.einsum("htk,thd->kd", dscores_low, query_block) * score_scale
        value_grad = jnp.einsum("htk,thd->kd", probs_low, grad_block)
        sink_kgrad = jnp.einsum("hts,thd->sd", sink_ds_low, query_block) * score_scale
        sink_vgrad = jnp.einsum("hts,thd->sd", sink_probs_low, grad_block)
        current = lax.dynamic_slice_in_dim(grad_store, begin, key_count, 0)
        grad_store = lax.dynamic_update_slice_in_dim(grad_store, current + jnp.concatenate([key_grad, value_grad], axis=1), begin, 0)
        sink_grad = sink_grad + jnp.concatenate([sink_kgrad, sink_vgrad], axis=1)
        return (grad_store, sink_grad), query_grad.reshape(TOK_DEV, H * DH)

    start_state = (jnp.zeros((TOKENS + reach_count * TOK_DEV, 2 * DH), jnp.float32), jnp.zeros((SINK, 2 * DH), jnp.float32))
    (grad_store, sink_grad), query_grads = lax.scan(one_block, start_state, jnp.arange(block_count, dtype=jnp.int32))
    query_grad = query_grads.reshape(TOKENS, H * DH)
    pair_grad = grad_store[reach_count * TOK_DEV:]
    return query_grad, pair_grad[:, :DH], pair_grad[:, DH:], sink_grad[:, :DH], sink_grad[:, DH:]
```

```python
import functools
import math

import jax
import jax.numpy as jnp
from jax import lax
from jax.experimental import pallas as pl
from jax.experimental.pallas import tpu as pltpu
from jax.sharding import PartitionSpec as P

WIN = 2048
AXES = ("seqhi", "seqlo")
LOG2E = math.log2(math.e)
NT = (((1,), (1,)), ((), ()))
TN = (((0,), (0,)), ((), ()))
NN = (((1,), (0,)), ((), ()))
VMEM_BYTES = 24 * 1024 * 1024


def dot(left, right, dims):
    return lax.dot_general(left, right, dims, preferred_element_type=jnp.float32)


def shifted(block, distance):
    count = lax.axis_size(AXES)
    route = [(i - distance, i) for i in range(count) if 0 <= i - distance < count]
    return lax.ppermute(block, AXES, route)


def exchange_sum(block):
    for axis in ("seqlo", "seqhi"):
        count = lax.axis_size(axis)
        if count & (count - 1):
            block = lax.psum(block, axis)
            continue
        step = 1
        while step < count:
            block = block + lax.ppermute(block, axis, [(i, i ^ step) for i in range(count)])
            step *= 2
    return block


def tile_grads(query, grad, key, value, lse_row, delta_row, scale, keep=None):
    scores = dot(key, query, NT)
    probs = jnp.exp2(scores * (scale * LOG2E) - lse_row)
    if keep is not None:
        probs = jnp.where(keep, probs, 0.0)
    dprobs = dot(value, grad, NT)
    dscores = probs * (dprobs - delta_row)
    probs_low = probs.astype(jnp.bfloat16)
    dscores_low = dscores.astype(jnp.bfloat16)
    value_grad = dot(probs_low, grad, NN)
    key_grad = dot(dscores_low, query, NN)
    query_grad = dot(dscores_low, key, TN)
    return query_grad, key_grad, value_grad


def own_kernel(
    window_ref, live_ref, query_ref, grad_ref, out_ref, lse_ref, pair_ref, sink_ref,
    dquery_ref, delta_ref, pair_grad_ref, sink_grad_ref,
    *, heads, width, scale,
):
    rows = query_ref.shape[0]
    sinks = sink_ref.shape[0]
    pair_grad_ref[...] = jnp.zeros_like(pair_grad_ref)
    sink_grad_ref[...] = jnp.zeros_like(sink_grad_ref)
    key_at = lax.broadcasted_iota(jnp.int32, (rows, rows), 0)
    query_at = lax.broadcasted_iota(jnp.int32, (rows, rows), 1)
    apart = query_at - key_at
    sink_at = lax.broadcasted_iota(jnp.int32, (sinks, rows), 0)

    def one_head(head, carry):
        lanes = pl.ds(pl.multiple_of(head * width, width), width)
        query = query_ref[:, lanes]
        grad = grad_ref[:, lanes]
        product = grad.astype(jnp.float32) * out_ref[:, lanes].astype(jnp.float32)
        delta_row = jnp.sum(product.T, axis=0, keepdims=True)
        delta_ref[pl.ds(head, 1), :] = delta_row
        lse_row = lse_ref[pl.ds(head, 1), :] * LOG2E
        keep = (apart >= 0) & (apart < window_ref[head])
        dquery, dkey, dvalue = tile_grads(
            query, grad, pair_ref[:, :width], pair_ref[:, width:], lse_row, delta_row, scale, keep
        )
        pair_grad_ref[:, :width] += dkey * scale
        pair_grad_ref[:, width:] += dvalue
        sink_keep = sink_at < live_ref[head]
        sink_dquery, dkey, dvalue = tile_grads(
            query, grad, sink_ref[:, :width], sink_ref[:, width:], lse_row, delta_row, scale, sink_keep
        )
        sink_grad_ref[:, :width] += dkey * scale
        sink_grad_ref[:, width:] += dvalue
        dquery_ref[:, lanes] = (dquery + sink_dquery) * scale
        return carry

    lax.fori_loop(0, heads, one_head, 0)


def far_kernel(
    window_ref, device_ref, query_ref, grad_ref, lse_ref, delta_ref, dquery_in, *rest,
    distances, heads, width, scale,
):
    count = len(distances)
    pair_refs = rest[:count]
    dquery_ref = rest[count]
    out_refs = rest[count + 1 : 2 * count + 1]
    sum_refs = rest[2 * count + 1 :]
    rows = query_ref.shape[0]
    dquery_ref[...] = dquery_in[...]
    for slot, distance in enumerate(distances):
        pair_ref, sum_ref = pair_refs[slot], sum_refs[slot]
        sum_ref[...] = jnp.zeros_like(sum_ref)

        def one_tile(head, masked, pair_ref=pair_ref, sum_ref=sum_ref, distance=distance):
            lanes = pl.ds(pl.multiple_of(head * width, width), width)
            keep = None
            if masked:
                key_at = lax.broadcasted_iota(jnp.int32, (rows, rows), 0)
                query_at = lax.broadcasted_iota(jnp.int32, (rows, rows), 1)
                keep = query_at - key_at < window_ref[head] - distance * rows
            dquery, dkey, dvalue = tile_grads(
                query_ref[:, lanes],
                grad_ref[:, lanes],
                pair_ref[:, :width],
                pair_ref[:, width:],
                lse_ref[pl.ds(head, 1), :] * LOG2E,
                delta_ref[pl.ds(head, 1), :],
                scale,
                keep,
            )
            sum_ref[:, :width] += dkey * scale
            sum_ref[:, width:] += dvalue
            dquery_ref[:, lanes] += dquery * scale

        @pl.when(device_ref[0] >= distance)
        def _(distance=distance, one_tile=one_tile):
            def one_head(head, carry):
                window = window_ref[head]
                inside = distance * rows + rows - 1 < window
                touched = distance * rows - rows + 1 < window
                pl.when(inside)(functools.partial(one_tile, head, False))
                pl.when(touched & jnp.logical_not(inside))(functools.partial(one_tile, head, True))
                return carry

            lax.fori_loop(0, heads, one_head, 0)

        out_refs[slot][...] = sum_ref[...].astype(jnp.bfloat16)


def cost(rows, keys, heads, width):
    tiles = rows * keys * heads
    return pl.CostEstimate(flops=10 * tiles * width, bytes_accessed=6 * rows * heads * width, transcendentals=tiles)


def on_device(
    queries, keys, values, outputs, out_grad, lse, sink_keys, sink_values, window_len, sink_live
):
    rows = queries.shape[0]
    heads = lse.shape[0]
    width = keys.shape[1]
    sinks = sink_keys.shape[0]
    reach = WIN // rows
    scale = width ** (-0.5)
    vmem = pl.BlockSpec(memory_space=pltpu.VMEM)
    smem = pl.BlockSpec(memory_space=pltpu.SMEM)
    device = lax.axis_index(AXES).astype(jnp.int32).reshape(1)
    own_pair = jnp.concatenate([keys, values], axis=1)
    sink_pair = jnp.concatenate([sink_keys, sink_values], axis=1)
    groups = [(8, 4), (2, 6), (1, 7), (3, 5)] if reach == 8 else [(d,) for d in range(1, reach + 1)]
    arrived = {d: shifted(own_pair, d) for group in groups for d in group}

    dquery, delta, pair_grad, sink_grad = pl.pallas_call(
        functools.partial(own_kernel, heads=heads, width=width, scale=scale),
        out_shape=(
            jax.ShapeDtypeStruct((rows, heads * width), jnp.float32),
            jax.ShapeDtypeStruct((heads, rows), jnp.float32),
            jax.ShapeDtypeStruct((rows, 2 * width), jnp.float32),
            jax.ShapeDtypeStruct((sinks, 2 * width), jnp.float32),
        ),
        in_specs=[smem] * 2 + [vmem] * 6,
        out_specs=(vmem,) * 4,
        compiler_params=pltpu.CompilerParams(vmem_limit_bytes=VMEM_BYTES),
        cost_estimate=cost(rows, rows + sinks, heads, width),
        name="own_and_sink",
    )(window_len, sink_live, queries, out_grad, outputs, lse, own_pair, sink_pair)

    sink_total = exchange_sum(sink_grad)
    returned = []
    for group in groups:
        results = pl.pallas_call(
            functools.partial(far_kernel, distances=group, heads=heads, width=width, scale=scale),
            out_shape=(jax.ShapeDtypeStruct((rows, heads * width), jnp.float32),)
            + tuple(jax.ShapeDtypeStruct((rows, 2 * width), jnp.bfloat16) for _ in group),
            in_specs=[smem] * 2 + [vmem] * (5 + len(group)),
            out_specs=(vmem,) * (1 + len(group)),
            scratch_shapes=[pltpu.VMEM((rows, 2 * width), jnp.float32) for _ in group],
            input_output_aliases={6: 0},
            compiler_params=pltpu.CompilerParams(vmem_limit_bytes=VMEM_BYTES),
            cost_estimate=cost(rows, rows * len(group), heads, width),
            name="far_" + "_".join(str(d) for d in group),
        )(window_len, device, queries, out_grad, lse, delta, dquery, *[arrived[d] for d in group])
        dquery = results[0]
        for distance, block in zip(group, results[1:]):
            returned.append(shifted(block, -distance))
    for block in returned:
        pair_grad = pair_grad + block.astype(jnp.float32)
    return (
        dquery,
        pair_grad[:, :width],
        pair_grad[:, width:],
        sink_total[:, :width],
        sink_total[:, width:],
    )


def solution(mesh):
    split = P(AXES, None)
    return jax.shard_map(
        on_device,
        mesh=mesh,
        in_specs=(split,) * 5 + (P(None, AXES),) + (P(),) * 4,
        out_specs=(split,) * 3 + (P(),) * 2,
        check_vma=False,
    )
```

```python
import functools
import math

import jax
import jax.numpy as jnp
from jax import lax
from jax.experimental import pallas as pl
from jax.experimental.pallas import tpu as pltpu
from jax.sharding import PartitionSpec as P

WIN = 2048
AXES = ("seqhi", "seqlo")
LOG2E = math.log2(math.e)
NN = (((1,), (0,)), ((), ()))
NT = (((1,), (1,)), ((), ()))
VMEM_BYTES = 30 * 1024 * 1024
UNROLL = 4
LOW = jnp.bfloat16
VMEM = pl.BlockSpec(memory_space=pltpu.VMEM)
SMEM = pl.BlockSpec(memory_space=pltpu.SMEM)


def dot(left, right, dims=NN):
    return lax.dot_general(left, right, dims, preferred_element_type=jnp.float32)


def rotated(block, distance):
    count = lax.axis_size(AXES)
    return lax.ppermute(block, AXES, [(i, (i + distance) % count) for i in range(count)])


def exchange_sum(block):
    for axis in ("seqlo", "seqhi"):
        count = lax.axis_size(axis)
        if count & (count - 1):
            block = lax.psum(block, axis)
            continue
        step = 1
        while step < count:
            block = block + lax.ppermute(block, axis, [(i, i ^ step) for i in range(count)])
            step *= 2
    return block


def span(index, size):
    return pl.ds(pl.multiple_of(index * size, size), size)


def sink_kernel(
    live_ref, query_ref, grad_ref, out_ref, lse_ref, sink_ref,
    query_t_ref, grad_t_ref, delta_ref, dquery_ref, sink_grad_ref,
    *, heads, width, scale,
):
    rows = query_ref.shape[0]
    sinks = sink_ref.shape[0]
    key, value = sink_ref[:, :width], sink_ref[:, width:]
    key_t = key.T
    sink_grad_ref[...] = jnp.zeros_like(sink_grad_ref)

    def one_head(head):
        lanes = span(head, width)
        strip = span(head, width)
        query_t = query_ref[:, lanes].T
        grad_t = grad_ref[:, lanes].T
        query_t_ref[strip, :] = query_t
        grad_t_ref[strip, :] = grad_t
        product = grad_t.astype(jnp.float32) * out_ref[:, lanes].T.astype(jnp.float32)
        delta = jnp.sum(product, axis=0, keepdims=True)
        delta_ref[pl.ds(head, 1), :] = delta
        probs = jnp.exp2(dot(key, query_t) * (scale * LOG2E) - lse_ref[pl.ds(head, 1), :] * LOG2E)
        at = lax.broadcasted_iota(jnp.int32, (sinks, rows), 0)
        probs = jnp.where(at < live_ref[head], probs, 0.0)
        dscores = (probs * (dot(value, grad_t) - delta)).astype(LOW)
        sink_grad_ref[:width, :] += dot(query_t, dscores, NT) * scale
        sink_grad_ref[width:, :] += dot(grad_t, probs.astype(LOW), NT)
        dquery_ref[strip, :] = dot(key_t, dscores)

    def some_heads(step, carry):
        for part in range(2):
            one_head(2 * step + part)
        return carry

    lax.fori_loop(0, heads // 2, some_heads, 0)


def block_kernel(
    window_ref, device_ref, query_t_ref, grad_t_ref, lse_ref, delta_ref, dquery_in, *rest,
    distances, heads, width, scale, causal,
):
    count = len(distances)
    pair_refs = rest[:count]
    dquery_ref = rest[count]
    out_refs = rest[count + 1 : 2 * count + 1]
    items_ref, pair_ref, key_t_ref, sum_ref, total_ref = rest[2 * count + 1 : 2 * count + 6]
    low_refs = rest[2 * count + 6 :]
    rows = pair_ref.shape[1]
    for slot in range(count):
        pair_ref[slot] = pair_refs[slot][...]
        key_t_ref[slot] = pair_refs[slot][:, :width].T
    sum_ref[...] = jnp.zeros_like(sum_ref)
    if not causal:
        dquery_ref[...] = dquery_in[...]
    dtotal_ref = total_ref if causal else dquery_ref
    if causal:
        total_ref[...] = dquery_in[...]
    for ref in low_refs:
        ref[...] = jnp.zeros_like(ref)

    def list_items(slot, distance, found):
        def one_head(head, found):
            left = window_ref[head] - distance * rows
            needed = (left > 1 - rows) & (device_ref[0] >= distance)

            @pl.when(needed)
            def _():
                items_ref[0, found] = slot
                items_ref[1, found] = head
                items_ref[2, found] = left

            return found + needed.astype(jnp.int32)

        return lax.fori_loop(0, heads, one_head, found)

    found = 0
    for slot, distance in enumerate(distances):
        found = list_items(slot, distance, found)
    steps = lax.div(found + UNROLL - 1, UNROLL)

    def pad_item(index, carry):
        items_ref[0, index] = 0
        items_ref[1, index] = 0
        items_ref[2, index] = -rows
        return carry

    lax.fori_loop(found, steps * UNROLL, pad_item, 0)

    def produce(index, probs_ref, dscores_ref):
        slot, head, left = items_ref[0, index], items_ref[1, index], items_ref[2, index]
        strip = span(head, width)
        scores = dot(pair_ref[slot, :, :width], query_t_ref[strip, :])
        probs = jnp.exp2(scores * (scale * LOG2E) - lse_ref[pl.ds(head, 1), :] * LOG2E)
        key_at = lax.broadcasted_iota(jnp.int32, (rows, 1), 0)
        query_at = lax.broadcasted_iota(jnp.int32, (1, rows), 1)
        keep = query_at - left < key_at
        if causal:
            keep = keep & (key_at <= query_at)
        probs = jnp.where(keep, probs, 0.0)
        dprobs = dot(pair_ref[slot, :, width:], grad_t_ref[strip, :])
        probs_ref[...] = probs.astype(LOW)
        dscores_ref[...] = (probs * (dprobs - delta_ref[pl.ds(head, 1), :])).astype(LOW)

    def consume(index, probs_ref, dscores_ref):
        slot, head = items_ref[0, index], items_ref[1, index]
        strip = span(head, width)
        dscores = dscores_ref[...]
        sum_ref[slot, width:, :] += dot(grad_t_ref[strip, :], probs_ref[...], NT)
        sum_ref[slot, :width, :] += dot(query_t_ref[strip, :], dscores, NT)
        dtotal_ref[strip, :] += dot(key_t_ref[slot], dscores)

    buffers = (low_refs[:2], low_refs[2:])

    def some_items(step, carry):
        for part in range(UNROLL):
            index = step * UNROLL + part
            produce(index, *buffers[part % 2])
            consume(jnp.maximum(index - 1, 0), *buffers[(part + 1) % 2])
        return carry

    lax.fori_loop(0, steps, some_items, 0)

    @pl.when(found > 0)
    def _():
        consume(steps * UNROLL - 1, *buffers[(UNROLL - 1) % 2])

    for slot in range(count):
        out_refs[slot][:width, :] = (sum_ref[slot, :width, :] * scale).astype(out_refs[slot].dtype)
        out_refs[slot][width:, :] = sum_ref[slot, width:, :].astype(out_refs[slot].dtype)
    if causal:

        def turn(head, carry):
            dquery_ref[:, span(head, width)] = total_ref[span(head, width), :].T * scale
            return carry

        lax.fori_loop(0, heads, turn, 0)


def block_call(distances, heads, width, rows, causal, args, pairs):
    count = len(distances)
    wide = heads * width
    kind = jnp.float32 if causal else LOW
    dquery = (rows, wide) if causal else (wide, rows)
    return pl.pallas_call(
        functools.partial(
            block_kernel, distances=distances, heads=heads, width=width, scale=width**-0.5, causal=causal
        ),
        out_shape=(jax.ShapeDtypeStruct(dquery, jnp.float32),)
        + tuple(jax.ShapeDtypeStruct((2 * width, rows), kind) for _ in distances),
        in_specs=[SMEM] * 2 + [VMEM] * (5 + count),
        out_specs=(VMEM,) * (1 + count),
        scratch_shapes=[
            pltpu.SMEM((3, count * heads + UNROLL), jnp.int32),
            pltpu.VMEM((count, rows, 2 * width), LOW),
            pltpu.VMEM((count, width, rows), LOW),
            pltpu.VMEM((count, 2 * width, rows), jnp.float32),
            pltpu.VMEM((wide, rows) if causal else (8, rows), jnp.float32),
        ]
        + [pltpu.VMEM((rows, rows), LOW)] * 4,
        compiler_params=pltpu.CompilerParams(vmem_limit_bytes=VMEM_BYTES),
        cost_estimate=pl.CostEstimate(flops=1, bytes_accessed=1, transcendentals=0),
        name="blocks_" + "_".join(str(d) for d in distances),
    )(*args, *pairs)


def join_kernel(own_ref, *rest, width):
    key_ref, value_ref = rest[-2:]
    total = own_ref[...]
    for ref in rest[:-2]:
        total = total + ref[...].astype(jnp.float32)
    turned = total.T
    key_ref[...] = turned[:, :width]
    value_ref[...] = turned[:, width:]


def on_device(
    queries, keys, values, outputs, out_grad, lse, sink_keys, sink_values, window_len, sink_live
):
    rows = queries.shape[0]
    heads = lse.shape[0]
    width = keys.shape[1]
    sinks = sink_keys.shape[0]
    wide = heads * width
    reach = WIN // rows
    device = lax.axis_index(AXES).astype(jnp.int32).reshape(1)
    own_pair = jnp.concatenate([keys, values], axis=1)
    sink_pair = jnp.concatenate([sink_keys, sink_values], axis=1)
    order = [d for d in (2, 4, 6, 8, 1, 7, 3, 5) if d <= reach]
    order += [d for d in range(1, reach + 1) if d not in order]
    groups = [tuple(order[i : i + 2]) for i in range(0, len(order), 2)]
    arrived = {d: rotated(own_pair, d) for d in order}

    query_t, grad_t, delta, dquery, sink_grad = pl.pallas_call(
        functools.partial(sink_kernel, heads=heads, width=width, scale=width**-0.5),
        out_shape=(
            jax.ShapeDtypeStruct((wide, rows), LOW),
            jax.ShapeDtypeStruct((wide, rows), LOW),
            jax.ShapeDtypeStruct((heads, rows), jnp.float32),
            jax.ShapeDtypeStruct((wide, rows), jnp.float32),
            jax.ShapeDtypeStruct((2 * width, sinks), jnp.float32),
        ),
        in_specs=[SMEM] + [VMEM] * 5,
        out_specs=(VMEM,) * 5,
        compiler_params=pltpu.CompilerParams(vmem_limit_bytes=VMEM_BYTES),
        cost_estimate=pl.CostEstimate(flops=1, bytes_accessed=1, transcendentals=0),
        name="sink_keys_part",
    )(sink_live, queries, out_grad, outputs, lse, sink_pair)

    sink_total = exchange_sum(sink_grad)
    returned = []
    for group in groups:
        args = (window_len, device, query_t, grad_t, lse, delta, dquery)
        results = block_call(group, heads, width, rows, False, args, [arrived[d] for d in group])
        dquery = results[0]
        for distance, block in zip(group, results[1:]):
            returned.append(rotated(block, -distance))
    args = (window_len, device, query_t, grad_t, lse, delta, dquery)
    dquery, own_grad = block_call((0,), heads, width, rows, True, args, [own_pair])
    key_grad, value_grad = pl.pallas_call(
        functools.partial(join_kernel, width=width),
        out_shape=(jax.ShapeDtypeStruct((rows, width), jnp.float32),) * 2,
        in_specs=[VMEM] * (1 + len(returned)),
        out_specs=(VMEM,) * 2,
        compiler_params=pltpu.CompilerParams(vmem_limit_bytes=VMEM_BYTES),
        name="join",
    )(own_grad, *returned)
    return (dquery, key_grad, value_grad, sink_total[:width].T, sink_total[width:].T)


def solution(mesh):
    split = P(AXES, None)
    return jax.shard_map(
        on_device,
        mesh=mesh,
        in_specs=(split,) * 5 + (P(None, AXES),) + (P(),) * 4,
        out_specs=(split,) * 3 + (P(),) * 2,
        check_vma=False,
    )
```

```python
import functools
import math

import jax
import jax.numpy as jnp
from jax import lax
from jax.experimental import pallas as pl
from jax.experimental.pallas import tpu as pltpu
from jax.sharding import PartitionSpec as P

WIN = 2048
AXES = ("seqhi", "seqlo")
LOG2E = math.log2(math.e)
NN = (((1,), (0,)), ((), ()))
NT = (((1,), (1,)), ((), ()))
VMEM_BYTES = 22 * 1024 * 1024
UNROLL = 4
LOW = jnp.bfloat16
VMEM = pl.BlockSpec(memory_space=pltpu.VMEM)
SMEM = pl.BlockSpec(memory_space=pltpu.SMEM)
HBM = pl.BlockSpec(memory_space=pltpu.HBM)
ANY = pl.BlockSpec(memory_space=pl.ANY)


def dot(left, right, dims=NN):
    return lax.dot_general(left, right, dims, preferred_element_type=jnp.float32)


def rotated(block, distance):
    count = lax.axis_size(AXES)
    return lax.ppermute(block, AXES, [(i, (i + distance) % count) for i in range(count)])


def swapped(block, move):
    flips = dict.fromkeys(AXES, 0)
    for axis, step in move:
        flips[axis] ^= step
    sizes = [lax.axis_size(axis) for axis in AXES]
    route = []
    for i in range(sizes[0] * sizes[1]):
        high, low = divmod(i, sizes[1])
        route.append((i, (high ^ flips[AXES[0]]) * sizes[1] + (low ^ flips[AXES[1]])))
    return lax.ppermute(block, AXES, route)


def exchange_rounds():
    rounds = []
    for axis in AXES:
        step = 1
        while step < lax.axis_size(axis):
            rounds.append((axis, step))
            step *= 2
    return rounds


def span(index, size):
    return pl.ds(pl.multiple_of(index * size, size), size)


def sink_kernel(
    table_ref, key_ref, value_ref, query_ref, grad_ref, out_ref, lse_in, sink_key_ref, sink_value_ref,
    turned_ref, row_ref, dquery_ref, sink_grad_ref, own_ref,
    *, heads, width, scale,
):
    rows = query_ref.shape[0]
    sinks = sink_key_ref.shape[0]
    sink_grad_ref[...] = jnp.zeros_like(sink_grad_ref)
    own_ref[:, :width] = key_ref[...]
    own_ref[:, width:] = value_ref[...]
    row_ref[:heads, :] = lse_in[...] * LOG2E
    key, value = sink_key_ref[...], sink_value_ref[...]
    key_t = key.T

    def one_head(head):
        strip = span(head, width)
        query_t = query_ref[:, strip].T
        grad_t = grad_ref[:, strip].T
        turned_ref[strip, :] = query_t
        turned_ref[span(heads + head, width), :] = grad_t
        product = grad_t.astype(jnp.float32) * out_ref[:, strip].T.astype(jnp.float32)
        delta = jnp.sum(product, axis=0, keepdims=True)
        row_ref[pl.ds(heads + head, 1), :] = delta
        probs = jnp.exp2(dot(key, query_t) * (scale * LOG2E) - row_ref[pl.ds(head, 1), :])
        at = lax.broadcasted_iota(jnp.int32, (sinks, rows), 0)
        probs = jnp.where(at < table_ref[heads + head], probs, 0.0)
        dscores = (probs * (dot(value, grad_t) - delta)).astype(LOW)
        sink_grad_ref[:width, :] += dot(query_t, dscores, NT) * scale
        sink_grad_ref[width:, :] += dot(grad_t, probs.astype(LOW), NT)
        dquery_ref[strip, :] = dot(key_t, dscores)

    def some_heads(step, carry):
        for part in range(UNROLL):
            one_head(UNROLL * step + part)
        return carry

    lax.fori_loop(0, heads // UNROLL, some_heads, 0)


def sum_of(refs):
    total = refs[0][...].astype(jnp.float32)
    for ref in refs[1:]:
        total = total + ref[...].astype(jnp.float32)
    return total


def mark_kernel(window_ref, live_ref, device_ref, block_ref, table_ref, same_ref):
    heads = window_ref.shape[0]
    for head in range(heads):
        table_ref[head] = window_ref[head]
        table_ref[heads + head] = live_ref[head]
    table_ref[2 * heads] = device_ref[0]


def fold_kernel(device_ref, first_ref, second_ref, other_ref, *refs, rows, terms, odd_only):
    outs = refs[terms:]
    outs[0][...] = (first_ref[...] + other_ref[:, :rows].astype(jnp.float32)).astype(LOW)
    other = other_ref[:, rows:].astype(jnp.float32)
    if odd_only:
        odd = jnp.full(other.shape, device_ref[device_ref.shape[0] - 1] & 1, jnp.int32) == 1
        other = jnp.where(odd, other, 0.0)
    outs[1][...] = (second_ref[...] + other).astype(LOW)
    if terms:
        outs[2][...] = sum_of(refs[:terms]).astype(LOW)


def send_kernel(device_ref, own_ref, two_ref, four_ref, six_ref, eight_ref, *refs):
    near_ref, far_ref, sum_ref = refs[-3:]
    rows = own_ref.shape[0]
    odd = jnp.full(own_ref.shape, device_ref[device_ref.shape[0] - 1] & 1, jnp.int32) == 1
    near_ref[:rows, :] = two_ref[...]
    near_ref[rows:, :] = four_ref[...]
    far_ref[:rows, :] = six_ref[...]
    far_ref[rows:, :] = jnp.where(odd, eight_ref[...], own_ref[...])
    sum_ref[...] = sum_of(refs[:-3])


def local(distances, device):
    return [
        jnp.where(device & 1 == 1, distance[1], distance[0]) if isinstance(distance, tuple) else distance
        for distance in distances
    ]


def block_kernel(*refs, layout, groups, heads, width, scale):
    refs = list(refs)

    def take(count):
        taken = refs[:count]
        del refs[:count]
        return taken

    pairs, sink_count, back_count, joined, last = layout
    table_ref, turned_ref, row_ref = take(3)
    device = table_ref[2 * heads]
    distances = local([distance for pair in pairs for distance in pair], device)
    pair_refs = take(len(pairs))
    sink_refs = take(sink_count)
    back_refs = take(back_count)
    part_refs = take(1 + len(groups)) if last else []
    take(1)
    dquery_ref = take(1)[0]
    out_refs = take(1 if joined else len(distances))
    sink_out_refs = take(1 if sink_count else 0)
    items_ref, pair_ref, key_t_ref, sum_ref = take(4)
    low_refs = take(4)
    total_ref, total_sems = take(2) if last else (None, None)
    rows = pair_ref.shape[1]

    slot = 0
    for ref, members in zip(pair_refs, pairs):
        for place in range(len(members)):
            block = ref[place * rows : (place + 1) * rows, :]
            pair_ref[slot] = block
            key_t_ref[slot] = block[:, :width].T
            slot += 1
    sum_ref[...] = jnp.zeros_like(sum_ref)
    for ref in low_refs:
        ref[...] = jnp.zeros_like(ref)

    def needed(head, distance):
        return (table_ref[head] - distance * rows > 1 - rows) & (device >= distance)

    def list_head(head, found):
        before = found
        for slot, distance in enumerate(distances):
            items_ref[0, found] = slot
            items_ref[1, found] = head
            items_ref[2, found] = table_ref[head] - distance * rows
            items_ref[3, found] = (found == before).astype(jnp.int32)
            found = found + needed(head, distance).astype(jnp.int32)
        return found

    found = lax.fori_loop(0, heads, list_head, 0)
    steps = lax.div(found + UNROLL - 1, UNROLL)

    def pad_item(index, carry):
        items_ref[0, index] = 0
        items_ref[1, index] = 0
        items_ref[2, index] = -rows
        items_ref[3, index] = 0
        return carry

    lax.fori_loop(found, steps * UNROLL, pad_item, 0)

    def produce(index, probs_ref, dscores_ref):
        slot, head, left = items_ref[0, index], items_ref[1, index], items_ref[2, index]
        strip = span(head, width)
        scores = dot(pair_ref[slot, :, :width], turned_ref[strip, :])
        probs = jnp.exp2(scores * (scale * LOG2E) - row_ref[pl.ds(head, 1), :])
        key_at = lax.broadcasted_iota(jnp.int32, (rows, 1), 0)
        query_at = lax.broadcasted_iota(jnp.int32, (1, rows), 1)
        keep = query_at - left < key_at
        if last:
            keep = keep & (key_at <= query_at)
        probs = jnp.where(keep, probs, 0.0)
        dprobs = dot(pair_ref[slot, :, width:], turned_ref[span(heads + head, width), :])
        probs_ref[...] = probs.astype(LOW)
        dscores_ref[...] = (probs * (dprobs - row_ref[pl.ds(heads + head, 1), :])).astype(LOW)

    def consume(index, probs_ref, dscores_ref):
        slot, head = items_ref[0, index], items_ref[1, index]
        strip = span(head, width)
        dscores = dscores_ref[...]
        sum_ref[slot, width:, :] += dot(turned_ref[span(heads + head, width), :], probs_ref[...], NT)
        sum_ref[slot, :width, :] += dot(turned_ref[strip, :], dscores, NT)
        dquery = dot(key_t_ref[slot], dscores)
        if last:
            dquery = dquery + part_refs[0][strip, :]
            for ref, group in zip(part_refs[1:], groups):
                touched = functools.reduce(jnp.logical_or, [needed(head, distance) for distance in local(group, device)])
                dquery = dquery + jnp.where(touched, ref[strip, :], 0.0)
            total_ref[:, strip] = dquery.T * scale
        else:
            dquery_ref[strip, :] = dquery + jnp.where(items_ref[3, index] == 1, 0.0, dquery_ref[strip, :])

    buffers = (low_refs[:2], low_refs[2:])

    def total_copy(step):
        lanes = span(step, UNROLL * width)
        return pltpu.make_async_copy(total_ref.at[:, lanes], dquery_ref.at[:, lanes], total_sems.at[step])

    def some_items(step, carry):
        for part in range(UNROLL):
            index = step * UNROLL + part
            produce(index, *buffers[part % 2])
            consume(jnp.maximum(index - 1, 0), *buffers[(part + 1) % 2])
        if last:
            pl.when(step > 0)(lambda: total_copy(step - 1).start())
        return carry

    lax.fori_loop(0, steps, some_items, 0)

    @pl.when(found > 0)
    def _():
        consume(steps * UNROLL - 1, *buffers[(UNROLL - 1) % 2])

    if last:
        total_copy(heads // UNROLL - 1).start()
    for slot in range(len(distances)):
        grads = (sum_ref[slot, :width, :] * scale, sum_ref[slot, width:, :])
        for half, grad in enumerate(grads):
            strip = slice(half * width, (half + 1) * width)
            for ref in back_refs:
                grad = grad + ref[strip, :].astype(jnp.float32)
            if joined:
                out_refs[0][strip, slot * rows : (slot + 1) * rows] = grad.astype(out_refs[0].dtype)
            else:
                out_refs[slot][strip, :] = grad.astype(out_refs[slot].dtype)
    if sink_count:
        sink_out_refs[0][...] = sum_of(sink_refs)
    if last:
        for step in range(heads // UNROLL):
            total_copy(step).wait()


def block_call(pairs, pair_arrays, shared, after, sinks=(), backs=(), parts=(), groups=(), last=False, kind=LOW, joined=False):
    table, turned, row_terms = shared
    wide, rows = turned.shape[0] // 2, turned.shape[1]
    heads = row_terms.shape[0] // 2
    width = wide // heads
    distances = [distance for pair in pairs for distance in pair]
    count = len(distances)
    shape = jax.ShapeDtypeStruct
    outs = [shape((rows, wide) if last else (wide, rows), jnp.float32)]
    outs += [shape((2 * width, count * rows), kind)] if joined else [shape((2 * width, rows), kind)] * count
    if sinks:
        outs.append(shape(sinks[0].shape, jnp.float32))
    arrays = [turned, row_terms, *pair_arrays, *sinks, *backs, *parts, after]
    layout = (pairs, len(sinks), len(backs), joined, last)
    return pl.pallas_call(
        functools.partial(
            block_kernel, layout=layout, groups=groups, heads=heads, width=width, scale=width**-0.5
        ),
        out_shape=outs,
        in_specs=[SMEM] + [VMEM] * (len(arrays) - 1) + [ANY],
        out_specs=[HBM if last else VMEM] + [VMEM] * (len(outs) - 1),
        scratch_shapes=[
            pltpu.SMEM((4, count * heads + UNROLL), jnp.int32),
            pltpu.VMEM((count, rows, 2 * width), LOW),
            pltpu.VMEM((count, width, rows), LOW),
            pltpu.VMEM((count, 2 * width, rows), jnp.float32),
        ]
        + [pltpu.VMEM((rows, rows), LOW)] * 4
        + ([pltpu.VMEM((rows, wide), jnp.float32), pltpu.SemaphoreType.DMA((heads // UNROLL,))] if last else []),
        compiler_params=pltpu.CompilerParams(vmem_limit_bytes=VMEM_BYTES),
        cost_estimate=pl.CostEstimate(
            flops=10 * count * rows * rows * wide, bytes_accessed=2 * rows * wide, transcendentals=0
        ),
        name="blocks_" + "_".join(str(d[0] if isinstance(d, tuple) else d) for d in distances),
    )(table, *arrays)


def join_kernel(device_ref, own_ref, other_ref, *refs, backs, width):
    key_ref, value_ref, sink_key_ref, sink_value_ref = refs[-4:]
    rows = own_ref.shape[1]
    odd = jnp.full(own_ref.shape, device_ref[device_ref.shape[0] - 1] & 1, jnp.int32) == 1
    total = own_ref[...] + jnp.where(odd, 0.0, other_ref[:, rows:].astype(jnp.float32))
    turned = (total + sum_of(refs[:backs])).T
    key_ref[...] = turned[:, :width]
    value_ref[...] = turned[:, width:]
    turned = sum_of(refs[backs:-4]).T
    sink_key_ref[...] = turned[:, :width]
    sink_value_ref[...] = turned[:, width:]


def on_device(
    queries, keys, values, outputs, out_grad, lse, sink_keys, sink_values, window_len, sink_live
):
    rows = queries.shape[0]
    heads = lse.shape[0]
    width = keys.shape[1]
    sinks = sink_keys.shape[0]
    wide = heads * width
    shape = jax.ShapeDtypeStruct
    device = lax.axis_index(AXES).astype(jnp.int32).reshape(1)
    own_pair = jnp.concatenate([keys, values], axis=1)
    table, own_pair = pl.pallas_call(
        mark_kernel,
        out_shape=(shape((2 * heads + 1,), jnp.int32), shape(own_pair.shape, LOW)),
        in_specs=[SMEM] * 3 + [ANY],
        out_specs=(SMEM, ANY),
        input_output_aliases={3: 1},
        compiler_params=pltpu.CompilerParams(vmem_limit_bytes=1024 * 1024),
        cost_estimate=pl.CostEstimate(flops=2 * 10**10, bytes_accessed=1, transcendentals=0),
        name="mark",
    )(window_len, sink_live, device, own_pair)
    even = {d: rotated(own_pair, d) for d in (2, 4, 6, 8)}

    turned, row_terms, dquery, sink_grad, own_held = pl.pallas_call(
        functools.partial(sink_kernel, heads=heads, width=width, scale=width**-0.5),
        out_shape=(
            shape((2 * wide, rows), LOW),
            shape((2 * heads, rows), jnp.float32),
            shape((wide, rows), jnp.float32),
            shape((2 * width, sinks), jnp.float32),
            shape((rows, 2 * width), LOW),
        ),
        in_specs=[SMEM] + [VMEM] * 8,
        out_specs=(VMEM,) * 5,
        compiler_params=pltpu.CompilerParams(vmem_limit_bytes=VMEM_BYTES),
        cost_estimate=pl.CostEstimate(flops=10**10, bytes_accessed=10**6, transcendentals=0),
        name="sink_keys_part",
    )(table, keys, values, queries, out_grad, outputs, lse, sink_keys, sink_values)

    rounds = exchange_rounds()

    def sink_terms(count):
        moves = [()]
        for _ in range(min(count, len(rounds))):
            here = rounds.pop(0)
            moves = moves + [move + (here,) for move in moves]
        return [sink_grad] + [swapped(sink_grad, move) for move in moves[1:]]

    near, far, sink_grad = pl.pallas_call(
        send_kernel,
        out_shape=(shape((2 * rows, 2 * width), LOW),) * 2 + (shape(sink_grad.shape, jnp.float32),),
        in_specs=[SMEM] + [VMEM] * (7 if rounds else 6),
        out_specs=(VMEM,) * 3,
        compiler_params=pltpu.CompilerParams(vmem_limit_bytes=VMEM_BYTES),
        name="send_blocks",
    )(table, own_held, even[2], even[4], even[6], even[8], *sink_terms(1))
    partner = ((AXES[-1], 1),)
    near_odd, far_odd = swapped(near, partner), swapped(far, partner)

    shared = (table, turned, row_terms)
    parts = [dquery]
    sums = sink_terms(2)
    full = jnp.float32
    near_pair, far_pair = ((1, 3), (3, 5)), ((5, 7), (7, 1))
    part, grad_2, grad_4 = block_call([(2,), (4,)], [even[2], even[4]], shared, dquery, kind=full)
    parts.append(part)

    part, odd, sink_grad = block_call([near_pair], [near_odd], shared, part, sinks=sums, joined=True)
    parts.append(part)
    sums = sink_terms(1)
    near_other = swapped(odd, partner)

    part, odd = block_call([far_pair], [far_odd], shared, part, joined=True)
    parts.append(part)
    far_other = swapped(odd, partner)

    part, grad_6, grad_8 = block_call([(6,), (8,)], [even[6], even[8]], shared, part, kind=full)
    parts.append(part)

    def fold(first, second, other, terms=(), odd_only=False):
        outs = [shape(first.shape, LOW)] * 2 + ([shape(sink_grad.shape, LOW)] if terms else [])
        return pl.pallas_call(
            functools.partial(fold_kernel, rows=rows, terms=len(terms), odd_only=odd_only),
            out_shape=outs,
            in_specs=[SMEM] + [VMEM] * (3 + len(terms)),
            out_specs=[VMEM] * len(outs),
            compiler_params=pltpu.CompilerParams(vmem_limit_bytes=VMEM_BYTES),
            name="fold",
        )(table, first, second, other, *terms)

    grad_2, grad_4, sink_grad = fold(grad_2, grad_4, near_other, sums)
    sums = sink_terms(1)
    backs = [rotated(grad_2, -2), rotated(grad_4, -4)]
    grad_6, grad_8 = fold(grad_6, grad_8, far_other, odd_only=True)
    backs += [rotated(grad_6, -6), rotated(grad_8, -8)]
    dquery, own_grad = block_call(
        [(0,)], [own_held], shared, grad_8, parts=parts, kind=full, last=True,
        groups=((2, 4), near_pair, far_pair, (6, 8)),
    )
    while rounds:
        sink_grad = sum(sums)
        sums = sink_terms(1)
    key_grad, value_grad, sink_key_grad, sink_value_grad = pl.pallas_call(
        functools.partial(join_kernel, backs=len(backs), width=width),
        out_shape=(shape((rows, width), jnp.float32),) * 2 + (shape((sinks, width), jnp.float32),) * 2,
        in_specs=[SMEM] + [VMEM] * (2 + len(backs) + len(sums)),
        out_specs=(VMEM,) * 4,
        compiler_params=pltpu.CompilerParams(vmem_limit_bytes=VMEM_BYTES),
        name="join",
    )(table, own_grad, far_other, *backs, *sums)
    return (dquery, key_grad, value_grad, sink_key_grad, sink_value_grad)


def solution(mesh):
    split = P(AXES, None)
    return jax.shard_map(
        on_device,
        mesh=mesh,
        in_specs=(split,) * 5 + (P(None, AXES),) + (P(),) * 4,
        out_specs=(split,) * 3 + (P(),) * 2,
        check_vma=False,
    )
```

```python
import functools
import math

import jax
import jax.numpy as jnp
from jax import lax
from jax.experimental import pallas as pl
from jax.experimental.pallas import tpu as pltpu
from jax.sharding import PartitionSpec as P

WIN = 2048
AXES = ("seqhi", "seqlo")
LOG2E = math.log2(math.e)
NN = (((1,), (0,)), ((), ()))
NT = (((1,), (1,)), ((), ()))
VMEM_BYTES = 22 * 1024 * 1024
UNROLL = 4
LOW = jnp.bfloat16
VMEM = pl.BlockSpec(memory_space=pltpu.VMEM)
SMEM = pl.BlockSpec(memory_space=pltpu.SMEM)
HBM = pl.BlockSpec(memory_space=pltpu.HBM)
ANY = pl.BlockSpec(memory_space=pl.ANY)


def dot(left, right, dims=NN):
    return lax.dot_general(left, right, dims, preferred_element_type=jnp.float32)


def rotated(block, distance):
    count = lax.axis_size(AXES)
    return lax.ppermute(block, AXES, [(i, (i + distance) % count) for i in range(count)])


def swapped(block, move):
    flips = dict.fromkeys(AXES, 0)
    for axis, step in move:
        flips[axis] ^= step
    sizes = [lax.axis_size(axis) for axis in AXES]
    route = []
    for i in range(sizes[0] * sizes[1]):
        high, low = divmod(i, sizes[1])
        route.append((i, (high ^ flips[AXES[0]]) * sizes[1] + (low ^ flips[AXES[1]])))
    return lax.ppermute(block, AXES, route)


def exchange_rounds():
    rounds = []
    for axis in AXES:
        step = 1
        while step < lax.axis_size(axis):
            if axis != AXES[-1] or step > 4:
                rounds.append((axis, step))
            step *= 2
    return rounds


def span(index, size):
    return pl.ds(pl.multiple_of(index * size, size), size)


def sink_kernel(
    window_ref, live_ref, device_ref, key_ref, value_ref, query_ref, grad_ref, out_ref, lse_in, sink_key_ref, sink_value_ref,
    table_ref, turned_ref, row_ref, dquery_ref, sink_grad_ref, own_ref,
    *, heads, width, scale,
):
    rows = query_ref.shape[0]
    sinks = sink_key_ref.shape[0]
    sink_grad_ref[...] = jnp.zeros_like(sink_grad_ref)
    for head in range(heads):
        table_ref[head] = window_ref[head]
    table_ref[heads] = device_ref[0]
    own_ref[:, :width] = key_ref[...]
    own_ref[:, width:] = value_ref[...]
    row_ref[:heads, :] = lse_in[...] * LOG2E
    key, value = sink_key_ref[...], sink_value_ref[...]
    key_t = key.T

    def one_head(head):
        strip = span(head, width)
        query_t = query_ref[:, strip].T
        grad_t = grad_ref[:, strip].T
        turned_ref[strip, :] = query_t
        turned_ref[span(heads + head, width), :] = grad_t
        product = grad_t.astype(jnp.float32) * out_ref[:, strip].T.astype(jnp.float32)
        delta = jnp.sum(product, axis=0, keepdims=True)
        row_ref[pl.ds(heads + head, 1), :] = delta
        probs = jnp.exp2(dot(key, query_t) * (scale * LOG2E) - row_ref[pl.ds(head, 1), :])
        at = lax.broadcasted_iota(jnp.int32, (sinks, rows), 0)
        probs = jnp.where(at < live_ref[head], probs, 0.0)
        dscores = (probs * (dot(value, grad_t) - delta)).astype(LOW)
        sink_grad_ref[:width, :] += dot(query_t, dscores, NT) * scale
        sink_grad_ref[width:, :] += dot(grad_t, probs.astype(LOW), NT)
        dquery_ref[strip, :] = dot(key_t, dscores)

    def some_heads(step, carry):
        for part in range(UNROLL):
            one_head(UNROLL * step + part)
        return carry

    lax.fori_loop(0, heads // UNROLL, some_heads, 0)


def sum_of(refs):
    total = refs[0][...].astype(jnp.float32)
    for ref in refs[1:]:
        total = total + ref[...].astype(jnp.float32)
    return total


def mark_kernel(block_ref, same_ref):
    pass


def fold_kernel(table_ref, first_ref, second_ref, other_ref, *refs, rows, near):
    if near:
        mine_ref, first_out, second_out, sink_out = refs
        sinks = (mine_ref.shape[1] - 2 * rows) // 2
        sink = None
        for ref in (mine_ref, other_ref):
            high, low = ref[:, 2 * rows : 2 * rows + sinks], ref[:, 2 * rows + sinks :]
            whole = high.astype(jnp.float32) + low.astype(jnp.float32)
            sink = whole if sink is None else sink + whole
        sink = sink.astype(LOW)
        sink_out[...] = sink
        second_out[:, rows:] = sink
    else:
        sink_ref, first_out, second_out = refs
        sink = sink_ref[...]
    first_out[:, :rows] = (first_ref[...] + other_ref[:, :rows].astype(jnp.float32)).astype(LOW)
    first_out[:, rows:] = sink
    other = other_ref[:, rows : 2 * rows].astype(jnp.float32)
    if not near:
        odd = jnp.full(other.shape, table_ref[table_ref.shape[0] - 1] & 1, jnp.int32) == 1
        other = jnp.where(odd, other, 0.0)
    second_out[:, :rows] = (second_ref[...] + other).astype(LOW)


def near_kernel(two_ref, four_ref, *refs):
    near_ref, sum_ref = refs[-2:]
    rows = two_ref.shape[0]
    near_ref[:rows, :] = two_ref[...]
    near_ref[rows:, :] = four_ref[...]
    sum_ref[...] = sum_of(refs[:-2])


def far_kernel(table_ref, own_ref, six_ref, eight_ref, after_ref, far_ref):
    rows = own_ref.shape[0]
    odd = jnp.full(own_ref.shape, table_ref[table_ref.shape[0] - 1] & 1, jnp.int32) == 1
    far_ref[:rows, :] = six_ref[...]
    far_ref[rows:, :] = jnp.where(odd, eight_ref[...], own_ref[...])


def local(distances, device):
    return [
        jnp.where(device & 1 == 1, distance[1], distance[0]) if isinstance(distance, tuple) else distance
        for distance in distances
    ]


def block_kernel(*refs, layout, groups, heads, width, scale):
    refs = list(refs)

    def take(count):
        taken = refs[:count]
        del refs[:count]
        return taken

    pairs, sink_count, back_count, joined, last = layout
    table_ref, turned_ref, row_ref = take(3)
    device = table_ref[heads]
    distances = local([distance for pair in pairs for distance in pair], device)
    pair_refs = take(len(pairs))
    sink_refs = take(sink_count)
    back_refs = take(back_count)
    part_refs = take(1 + len(groups)) if last else []
    take(1)
    dquery_ref = take(1)[0]
    out_refs = take(1 if joined else len(distances))
    items_ref, pair_ref, key_t_ref, sum_ref = take(4)
    low_refs = take(4)
    total_ref, total_sems = take(2) if last else (None, None)
    rows = pair_ref.shape[1]

    slot = 0
    for ref, members in zip(pair_refs, pairs):
        for place in range(len(members)):
            block = ref[place * rows : (place + 1) * rows, :]
            pair_ref[slot] = block
            key_t_ref[slot] = block[:, :width].T
            slot += 1
    sum_ref[...] = jnp.zeros_like(sum_ref)
    for ref in low_refs:
        ref[...] = jnp.zeros_like(ref)

    def needed(head, distance):
        return (table_ref[head] - distance * rows > 1 - rows) & (device >= distance)

    def list_head(head, found):
        before = found
        for slot, distance in enumerate(distances):
            items_ref[0, found] = slot
            items_ref[1, found] = head
            items_ref[2, found] = table_ref[head] - distance * rows
            items_ref[3, found] = (found == before).astype(jnp.int32)
            found = found + needed(head, distance).astype(jnp.int32)
        return found

    found = lax.fori_loop(0, heads, list_head, 0)
    steps = lax.div(found + UNROLL - 1, UNROLL)

    def pad_item(index, carry):
        items_ref[0, index] = 0
        items_ref[1, index] = 0
        items_ref[2, index] = -rows
        items_ref[3, index] = 0
        return carry

    lax.fori_loop(found, steps * UNROLL, pad_item, 0)

    def produce(index, probs_ref, dscores_ref):
        slot, head, left = items_ref[0, index], items_ref[1, index], items_ref[2, index]
        strip = span(head, width)
        scores = dot(pair_ref[slot, :, :width], turned_ref[strip, :])
        probs = jnp.exp2(scores * (scale * LOG2E) - row_ref[pl.ds(head, 1), :])
        key_at = lax.broadcasted_iota(jnp.int32, (rows, 1), 0)
        query_at = lax.broadcasted_iota(jnp.int32, (1, rows), 1)
        keep = query_at - left < key_at
        if last:
            keep = keep & (key_at <= query_at)
        probs = jnp.where(keep, probs, 0.0)
        dprobs = dot(pair_ref[slot, :, width:], turned_ref[span(heads + head, width), :])
        probs_ref[...] = probs.astype(LOW)
        dscores_ref[...] = (probs * (dprobs - row_ref[pl.ds(heads + head, 1), :])).astype(LOW)

    def consume(index, probs_ref, dscores_ref):
        slot, head = items_ref[0, index], items_ref[1, index]
        strip = span(head, width)
        dscores = dscores_ref[...]
        sum_ref[slot, width:, :] += dot(turned_ref[span(heads + head, width), :], probs_ref[...], NT)
        sum_ref[slot, :width, :] += dot(turned_ref[strip, :], dscores, NT)
        dquery = dot(key_t_ref[slot], dscores)
        if last:
            dquery = dquery + part_refs[0][strip, :]
            for ref, group in zip(part_refs[1:], groups):
                touched = functools.reduce(jnp.logical_or, [needed(head, distance) for distance in local(group, device)])
                dquery = dquery + jnp.where(touched, ref[strip, :], 0.0)
            total_ref[:, strip] = dquery.T * scale
        else:
            dquery_ref[strip, :] = dquery + jnp.where(items_ref[3, index] == 1, 0.0, dquery_ref[strip, :])

    buffers = (low_refs[:2], low_refs[2:])

    def total_copy(step):
        lanes = span(step, UNROLL * width)
        return pltpu.make_async_copy(total_ref.at[:, lanes], dquery_ref.at[:, lanes], total_sems.at[step])

    def some_items(step, carry):
        for part in range(UNROLL):
            index = step * UNROLL + part
            produce(index, *buffers[part % 2])
            consume(jnp.maximum(index - 1, 0), *buffers[(part + 1) % 2])
        if last:
            pl.when(step > 0)(lambda: total_copy(step - 1).start())
        return carry

    lax.fori_loop(0, steps, some_items, 0)

    @pl.when(found > 0)
    def _():
        consume(steps * UNROLL - 1, *buffers[(UNROLL - 1) % 2])

    if last:
        total_copy(heads // UNROLL - 1).start()
    for slot in range(len(distances)):
        grads = (sum_ref[slot, :width, :] * scale, sum_ref[slot, width:, :])
        for half, grad in enumerate(grads):
            strip = slice(half * width, (half + 1) * width)
            for ref in back_refs:
                grad = grad + ref[strip, :].astype(jnp.float32)
            if joined:
                out_refs[0][strip, slot * rows : (slot + 1) * rows] = grad.astype(out_refs[0].dtype)
            else:
                out_refs[slot][strip, :] = grad.astype(out_refs[slot].dtype)
    if sink_count:
        total = sum_of(sink_refs)
        high = total.astype(LOW)
        sinks = total.shape[1]
        out_refs[0][:, len(distances) * rows : len(distances) * rows + sinks] = high
        out_refs[0][:, len(distances) * rows + sinks :] = (total - high.astype(jnp.float32)).astype(LOW)
    if last:
        for step in range(heads // UNROLL):
            total_copy(step).wait()


def block_call(pairs, pair_arrays, shared, after, sinks=(), backs=(), parts=(), groups=(), last=False, kind=LOW, joined=False):
    table, turned, row_terms = shared
    wide, rows = turned.shape[0] // 2, turned.shape[1]
    heads = row_terms.shape[0] // 2
    width = wide // heads
    distances = [distance for pair in pairs for distance in pair]
    count = len(distances)
    shape = jax.ShapeDtypeStruct
    outs = [shape((rows, wide) if last else (wide, rows), jnp.float32)]
    extra = 2 * sinks[0].shape[1] if sinks else 0
    outs += [shape((2 * width, count * rows + extra), kind)] if joined else [shape((2 * width, rows), kind)] * count
    arrays = [turned, row_terms, *pair_arrays, *sinks, *backs, *parts, after]
    layout = (pairs, len(sinks), len(backs), joined, last)
    return pl.pallas_call(
        functools.partial(
            block_kernel, layout=layout, groups=groups, heads=heads, width=width, scale=width**-0.5
        ),
        out_shape=outs,
        in_specs=[SMEM] + [VMEM] * (len(arrays) - 1) + [ANY],
        out_specs=[HBM if last else VMEM] + [VMEM] * (len(outs) - 1),
        scratch_shapes=[
            pltpu.SMEM((4, count * heads + UNROLL), jnp.int32),
            pltpu.VMEM((count, rows, 2 * width), LOW),
            pltpu.VMEM((count, width, rows), LOW),
            pltpu.VMEM((count, 2 * width, rows), jnp.float32),
        ]
        + [pltpu.VMEM((rows, rows), LOW)] * 4
        + ([pltpu.VMEM((rows, wide), jnp.float32), pltpu.SemaphoreType.DMA((heads // UNROLL,))] if last else []),
        compiler_params=pltpu.CompilerParams(vmem_limit_bytes=VMEM_BYTES),
        cost_estimate=pl.CostEstimate(
            flops=10 * count * rows * rows * wide, bytes_accessed=2 * rows * wide, transcendentals=0
        ),
        name="blocks_" + "_".join(str(d[0] if isinstance(d, tuple) else d) for d in distances),
    )(table, *arrays)


def join_kernel(
    table_ref, own_ref, other_ref, sink_ref, two_ref, four_ref, six_ref, eight_ref,
    key_ref, value_ref, sink_key_ref, sink_value_ref, *, width,
):
    rows = own_ref.shape[1]
    odd = jnp.full(own_ref.shape, table_ref[table_ref.shape[0] - 1] & 1, jnp.int32) == 1
    total = own_ref[...] + jnp.where(odd, 0.0, other_ref[:, rows:].astype(jnp.float32))
    for ref in (two_ref, four_ref, six_ref, eight_ref):
        total = total + ref[:, :rows].astype(jnp.float32)
    turned = total.T
    key_ref[...] = turned[:, :width]
    value_ref[...] = turned[:, width:]
    sums = [sink_ref[...]] + [ref[:, rows:] for ref in (two_ref, four_ref, six_ref)]
    sums = [term.astype(jnp.float32) for term in sums]
    turned = ((sums[0] + sums[2]) + (sums[1] + sums[3])).T
    sink_key_ref[...] = turned[:, :width]
    sink_value_ref[...] = turned[:, width:]


def on_device(
    queries, keys, values, outputs, out_grad, lse, sink_keys, sink_values, window_len, sink_live
):
    rows = queries.shape[0]
    heads = lse.shape[0]
    width = keys.shape[1]
    sinks = sink_keys.shape[0]
    wide = heads * width
    shape = jax.ShapeDtypeStruct
    device = lax.axis_index(AXES).astype(jnp.int32).reshape(1)
    own_pair = jnp.concatenate([keys, values], axis=1)
    own_pair = pl.pallas_call(
        mark_kernel,
        out_shape=shape(own_pair.shape, LOW),
        in_specs=[ANY],
        out_specs=ANY,
        input_output_aliases={0: 0},
        compiler_params=pltpu.CompilerParams(vmem_limit_bytes=1024 * 1024),
        cost_estimate=pl.CostEstimate(flops=2 * 10**10, bytes_accessed=1, transcendentals=0),
        name="mark",
    )(own_pair)
    even = {d: rotated(own_pair, d) for d in (8, 6, 4, 2)}

    table, turned, row_terms, dquery, sink_grad, own_held = pl.pallas_call(
        functools.partial(sink_kernel, heads=heads, width=width, scale=width**-0.5),
        out_shape=(
            shape((heads + 1,), jnp.int32),
            shape((2 * wide, rows), LOW),
            shape((2 * heads, rows), jnp.float32),
            shape((wide, rows), jnp.float32),
            shape((2 * width, sinks), jnp.float32),
            shape((rows, 2 * width), LOW),
        ),
        in_specs=[SMEM] * 3 + [VMEM] * 8,
        out_specs=(SMEM,) + (VMEM,) * 5,
        compiler_params=pltpu.CompilerParams(vmem_limit_bytes=VMEM_BYTES),
        cost_estimate=pl.CostEstimate(flops=10**10, bytes_accessed=10**6, transcendentals=0),
        name="sink_keys_part",
    )(window_len, sink_live, device, keys, values, queries, out_grad, outputs, lse, sink_keys, sink_values)

    rounds = exchange_rounds()

    def sink_terms():
        return [sink_grad] + ([swapped(sink_grad, (rounds.pop(0),))] if rounds else [])

    terms = sink_terms()
    near, sink_grad = pl.pallas_call(
        near_kernel,
        out_shape=(shape((2 * rows, 2 * width), LOW), shape(sink_grad.shape, jnp.float32)),
        in_specs=[VMEM] * (2 + len(terms)),
        out_specs=(VMEM,) * 2,
        compiler_params=pltpu.CompilerParams(vmem_limit_bytes=VMEM_BYTES),
        name="near_blocks",
    )(even[2], even[4], *terms)
    partner = ((AXES[-1], 1),)
    near_odd = swapped(near, partner)
    while len(rounds) > 1:
        sink_grad = sum(sink_terms())
    terms = sink_terms()

    shared = (table, turned, row_terms)
    parts = [dquery]
    full = jnp.float32
    near_pair, far_pair = ((1, 3), (3, 5)), ((5, 7), (7, 1))
    part, grad_2, grad_4 = block_call([(2,), (4,)], [even[2], even[4]], shared, near, kind=full)
    parts.append(part)

    far = pl.pallas_call(
        far_kernel,
        out_shape=shape((2 * rows, 2 * width), LOW),
        in_specs=[SMEM] + [VMEM] * 3 + [ANY],
        out_specs=VMEM,
        compiler_params=pltpu.CompilerParams(vmem_limit_bytes=VMEM_BYTES),
        name="far_blocks",
    )(table, own_held, even[6], even[8], part)
    far_odd = swapped(far, partner)

    part, near_mine = block_call([near_pair], [near_odd], shared, far, sinks=terms, joined=True)
    parts.append(part)
    near_other = swapped(near_mine, partner)

    part, far_mine = block_call([far_pair], [far_odd], shared, part, joined=True)
    parts.append(part)
    far_other = swapped(far_mine, partner)

    part, grad_6, grad_8 = block_call([(6,), (8,)], [even[6], even[8]], shared, part, kind=full)
    parts.append(part)

    def fold(first, second, other, extra, near):
        outs = [shape((2 * width, rows + sinks), LOW), shape((2 * width, rows + (sinks if near else 0)), LOW)]
        outs += [shape((2 * width, sinks), LOW)] if near else []
        return pl.pallas_call(
            functools.partial(fold_kernel, rows=rows, near=near),
            out_shape=outs,
            in_specs=[SMEM] + [VMEM] * 4,
            out_specs=[VMEM] * len(outs),
            compiler_params=pltpu.CompilerParams(vmem_limit_bytes=VMEM_BYTES),
            name="fold",
        )(table, first, second, other, extra)

    grad_2, grad_4, sink_low = fold(grad_2, grad_4, near_other, near_mine, True)
    backs = [rotated(grad_2, -2), rotated(grad_4, -4)]
    grad_6, grad_8 = fold(grad_6, grad_8, far_other, sink_low, False)
    backs += [rotated(grad_6, -6), rotated(grad_8, -8)]
    dquery, own_grad = block_call(
        [(0,)], [own_held], shared, grad_8, parts=parts, kind=full, last=True,
        groups=((2, 4), near_pair, far_pair, (6, 8)),
    )
    key_grad, value_grad, sink_key_grad, sink_value_grad = pl.pallas_call(
        functools.partial(join_kernel, width=width),
        out_shape=(shape((rows, width), jnp.float32),) * 2 + (shape((sinks, width), jnp.float32),) * 2,
        in_specs=[SMEM] + [VMEM] * 7,
        out_specs=(VMEM,) * 4,
        compiler_params=pltpu.CompilerParams(vmem_limit_bytes=VMEM_BYTES),
        name="join",
    )(table, own_grad, far_other, sink_low, *backs)
    return (dquery, key_grad, value_grad, sink_key_grad, sink_value_grad)


def solution(mesh):
    split = P(AXES, None)
    return jax.shard_map(
        on_device,
        mesh=mesh,
        in_specs=(split,) * 5 + (P(None, AXES),) + (P(),) * 4,
        out_specs=(split,) * 3 + (P(),) * 2,
        check_vma=False,
    )
```

```python
import functools
import math

import jax
import jax.numpy as jnp
from jax import lax
from jax.experimental import pallas as pl
from jax.experimental.pallas import tpu as pltpu
from jax.sharding import PartitionSpec as P

WIN = 2048
AXES = ("seqhi", "seqlo")
LOG2E = math.log2(math.e)
NN = (((1,), (0,)), ((), ()))
NT = (((1,), (1,)), ((), ()))
VMEM_BYTES = 22 * 1024 * 1024
UNROLL = 4
LOW = jnp.bfloat16
VMEM = pl.BlockSpec(memory_space=pltpu.VMEM)
SMEM = pl.BlockSpec(memory_space=pltpu.SMEM)
HBM = pl.BlockSpec(memory_space=pltpu.HBM)
ANY = pl.BlockSpec(memory_space=pl.ANY)


def dot(left, right, dims=NN):
    return lax.dot_general(left, right, dims, preferred_element_type=jnp.float32)


def rotated(block, distance):
    count = lax.axis_size(AXES)
    return lax.ppermute(block, AXES, [(i, (i + distance) % count) for i in range(count)])


def swapped(block, move):
    flips = dict.fromkeys(AXES, 0)
    for axis, step in move:
        flips[axis] ^= step
    sizes = [lax.axis_size(axis) for axis in AXES]
    route = []
    for i in range(sizes[0] * sizes[1]):
        high, low = divmod(i, sizes[1])
        route.append((i, (high ^ flips[AXES[0]]) * sizes[1] + (low ^ flips[AXES[1]])))
    return lax.ppermute(block, AXES, route)


def exchange_rounds():
    bits = {axis: [1 << bit for bit in range(lax.axis_size(axis).bit_length() - 1)] for axis in AXES}
    first, rest = bits[AXES[0]][:1], bits[AXES[0]][1:]
    low, high = bits[AXES[1]][:1], bits[AXES[1]][1:]
    order = [(AXES[0], first), (AXES[1], high), (AXES[1], low), (AXES[0], rest)]
    return [(axis, step) for axis, steps in order for step in steps]


def span(index, size):
    return pl.ds(pl.multiple_of(index * size, size), size)


def sink_kernel(
    window_ref, live_ref, device_ref, key_ref, value_ref, query_ref, grad_ref, out_ref, lse_in, sink_key_ref, sink_value_ref,
    table_ref, turned_ref, row_ref, dquery_ref, sink_grad_ref, own_ref,
    *, heads, width, scale,
):
    rows = query_ref.shape[0]
    sinks = sink_key_ref.shape[0]
    sink_grad_ref[...] = jnp.zeros_like(sink_grad_ref)
    for head in range(heads):
        table_ref[head] = window_ref[head]
    table_ref[heads] = device_ref[0]
    own_ref[:, :width] = key_ref[...]
    own_ref[:, width:] = value_ref[...]
    row_ref[:heads, :] = lse_in[...] * LOG2E
    key, value = sink_key_ref[...], sink_value_ref[...]
    key_t = key.T

    def one_head(head):
        strip = span(head, width)
        query_t = query_ref[:, strip].T
        grad_t = grad_ref[:, strip].T
        turned_ref[strip, :] = query_t
        turned_ref[span(heads + head, width), :] = grad_t
        product = grad_t.astype(jnp.float32) * out_ref[:, strip].T.astype(jnp.float32)
        delta = jnp.sum(product, axis=0, keepdims=True)
        row_ref[pl.ds(heads + head, 1), :] = delta
        probs = jnp.exp2(dot(key, query_t) * (scale * LOG2E) - row_ref[pl.ds(head, 1), :])
        at = lax.broadcasted_iota(jnp.int32, (sinks, rows), 0)
        probs = jnp.where(at < live_ref[head], probs, 0.0)
        dscores = (probs * (dot(value, grad_t) - delta)).astype(LOW)
        sink_grad_ref[:width, :] += dot(query_t, dscores, NT) * scale
        sink_grad_ref[width:, :] += dot(grad_t, probs.astype(LOW), NT)
        dquery_ref[strip, :] = dot(key_t, dscores)

    def some_heads(step, carry):
        for part in range(UNROLL):
            one_head(UNROLL * step + part)
        return carry

    lax.fori_loop(0, heads // UNROLL, some_heads, 0)


def sum_of(refs):
    total = refs[0][...].astype(jnp.float32)
    for ref in refs[1:]:
        total = total + ref[...].astype(jnp.float32)
    return total


def mark_kernel(block_ref, same_ref):
    pass


def fold_kernel(table_ref, first_ref, second_ref, other_ref, after_ref, *refs, near):
    first_out, second_out, sum_ref = refs[-3:]
    rows = first_ref.shape[1]
    first_out[...] = (first_ref[...] + other_ref[:, :rows].astype(jnp.float32)).astype(LOW)
    other = other_ref[:, rows:].astype(jnp.float32)
    if not near:
        odd = jnp.full(other.shape, table_ref[table_ref.shape[0] - 1] & 1, jnp.int32) == 1
        other = jnp.where(odd, other, 0.0)
    second_out[...] = (second_ref[...] + other).astype(LOW)
    sum_ref[...] = sum_of(refs[:-3])


def near_kernel(two_ref, four_ref, *refs):
    near_ref, sum_ref = refs[-2:]
    rows = two_ref.shape[0]
    near_ref[:rows, :] = two_ref[...]
    near_ref[rows:, :] = four_ref[...]
    sum_ref[...] = sum_of(refs[:-2])


def far_kernel(table_ref, own_ref, six_ref, eight_ref, after_ref, *refs):
    far_ref, sum_ref = refs[-2:]
    rows = own_ref.shape[0]
    odd = jnp.full(own_ref.shape, table_ref[table_ref.shape[0] - 1] & 1, jnp.int32) == 1
    far_ref[:rows, :] = six_ref[...]
    far_ref[rows:, :] = jnp.where(odd, eight_ref[...], own_ref[...])
    sum_ref[...] = sum_of(refs[:-2])


def local(distances, device):
    return [
        jnp.where(device & 1 == 1, distance[1], distance[0]) if isinstance(distance, tuple) else distance
        for distance in distances
    ]


def block_kernel(*refs, layout, groups, heads, width, scale):
    refs = list(refs)

    def take(count):
        taken = refs[:count]
        del refs[:count]
        return taken

    pairs, joined, last = layout
    table_ref, turned_ref, row_ref = take(3)
    device = table_ref[heads]
    distances = local([distance for pair in pairs for distance in pair], device)
    pair_refs = take(len(pairs))
    part_refs = take(1 + len(groups)) if last else []
    take(1)
    dquery_ref = take(1)[0]
    out_refs = take(1 if joined else len(distances))
    items_ref, pair_ref, key_t_ref, sum_ref = take(4)
    low_refs = take(4)
    total_ref, total_sems = take(2) if last else (None, None)
    rows = pair_ref.shape[1]
    unroll = UNROLL if last else 2 * UNROLL

    slot = 0
    for ref, members in zip(pair_refs, pairs):
        for place in range(len(members)):
            block = ref[place * rows : (place + 1) * rows, :]
            pair_ref[slot] = block
            key_t_ref[slot] = block[:, :width].T
            slot += 1
    sum_ref[...] = jnp.zeros_like(sum_ref)
    for ref in low_refs:
        ref[...] = jnp.zeros_like(ref)

    def needed(head, distance):
        return (table_ref[head] - distance * rows > 1 - rows) & (device >= distance)

    def list_head(head, found):
        before = found
        for slot, distance in enumerate(distances):
            items_ref[0, found] = slot
            items_ref[1, found] = head
            items_ref[2, found] = table_ref[head] - distance * rows
            items_ref[3, found] = (found == before).astype(jnp.int32)
            found = found + needed(head, distance).astype(jnp.int32)
        return found

    found = lax.fori_loop(0, heads, list_head, 0)
    steps = lax.div(found + unroll - 1, unroll)

    def pad_item(index, carry):
        items_ref[0, index] = 0
        items_ref[1, index] = 0
        items_ref[2, index] = -rows
        items_ref[3, index] = 0
        return carry

    lax.fori_loop(found, steps * unroll, pad_item, 0)

    def produce(index, probs_ref, dscores_ref):
        slot, head, left = items_ref[0, index], items_ref[1, index], items_ref[2, index]
        strip = span(head, width)
        scores = dot(pair_ref[slot, :, :width], turned_ref[strip, :])
        probs = jnp.exp2(scores * (scale * LOG2E) - row_ref[pl.ds(head, 1), :])
        key_at = lax.broadcasted_iota(jnp.int32, (rows, 1), 0)
        query_at = lax.broadcasted_iota(jnp.int32, (1, rows), 1)
        keep = query_at - left < key_at
        if last:
            keep = keep & (key_at <= query_at)
        probs = jnp.where(keep, probs, 0.0)
        dprobs = dot(pair_ref[slot, :, width:], turned_ref[span(heads + head, width), :])
        probs_ref[...] = probs.astype(LOW)
        dscores_ref[...] = (probs * (dprobs - row_ref[pl.ds(heads + head, 1), :])).astype(LOW)

    def consume(index, probs_ref, dscores_ref):
        slot, head = items_ref[0, index], items_ref[1, index]
        strip = span(head, width)
        dscores = dscores_ref[...]
        sum_ref[slot, width:, :] += dot(turned_ref[span(heads + head, width), :], probs_ref[...], NT)
        sum_ref[slot, :width, :] += dot(turned_ref[strip, :], dscores, NT)
        dquery = dot(key_t_ref[slot], dscores)
        if last:
            dquery = dquery + part_refs[0][strip, :]
            for ref, group in zip(part_refs[1:], groups):
                touched = functools.reduce(jnp.logical_or, [needed(head, distance) for distance in local(group, device)])
                dquery = dquery + jnp.where(touched, ref[strip, :], 0.0)
            total_ref[:, strip] = dquery.T * scale
        else:
            dquery_ref[strip, :] = dquery + jnp.where(items_ref[3, index] == 1, 0.0, dquery_ref[strip, :])

    buffers = (low_refs[:2], low_refs[2:])

    def total_copy(step):
        lanes = span(step, UNROLL * width)
        return pltpu.make_async_copy(total_ref.at[:, lanes], dquery_ref.at[:, lanes], total_sems.at[step])

    def some_items(step, carry):
        for part in range(unroll):
            index = step * unroll + part
            produce(index, *buffers[part % 2])
            consume(jnp.maximum(index - 1, 0), *buffers[(part + 1) % 2])
        if last:
            pl.when(step > 0)(lambda: total_copy(step - 1).start())
        return carry

    lax.fori_loop(0, steps, some_items, 0)

    @pl.when(found > 0)
    def _():
        consume(steps * unroll - 1, *buffers[(unroll - 1) % 2])

    if last:
        total_copy(heads // UNROLL - 1).start()
    for slot in range(len(distances)):
        grads = (sum_ref[slot, :width, :] * scale, sum_ref[slot, width:, :])
        for half, grad in enumerate(grads):
            strip = slice(half * width, (half + 1) * width)
            if joined:
                out_refs[0][strip, slot * rows : (slot + 1) * rows] = grad.astype(out_refs[0].dtype)
            else:
                out_refs[slot][strip, :] = grad.astype(out_refs[slot].dtype)
    if last:
        for step in range(heads // UNROLL):
            total_copy(step).wait()


def block_call(pairs, pair_arrays, shared, after, parts=(), groups=(), last=False, kind=LOW, joined=False):
    table, turned, row_terms = shared
    wide, rows = turned.shape[0] // 2, turned.shape[1]
    heads = row_terms.shape[0] // 2
    width = wide // heads
    distances = [distance for pair in pairs for distance in pair]
    count = len(distances)
    shape = jax.ShapeDtypeStruct
    outs = [shape((rows, wide) if last else (wide, rows), jnp.float32)]
    outs += [shape((2 * width, count * rows), kind)] if joined else [shape((2 * width, rows), kind)] * count
    arrays = [turned, row_terms, *pair_arrays, *parts, after]
    layout = (pairs, joined, last)
    return pl.pallas_call(
        functools.partial(
            block_kernel, layout=layout, groups=groups, heads=heads, width=width, scale=width**-0.5
        ),
        out_shape=outs,
        in_specs=[SMEM] + [VMEM] * (len(arrays) - 1) + [ANY],
        out_specs=[HBM if last else VMEM] + [VMEM] * (len(outs) - 1),
        scratch_shapes=[
            pltpu.SMEM((4, count * heads + 2 * UNROLL), jnp.int32),
            pltpu.VMEM((count, rows, 2 * width), LOW),
            pltpu.VMEM((count, width, rows), LOW),
            pltpu.VMEM((count, 2 * width, rows), jnp.float32),
        ]
        + [pltpu.VMEM((rows, rows), LOW)] * 4
        + ([pltpu.VMEM((rows, wide), jnp.float32), pltpu.SemaphoreType.DMA((heads // UNROLL,))] if last else []),
        compiler_params=pltpu.CompilerParams(vmem_limit_bytes=VMEM_BYTES),
        cost_estimate=pl.CostEstimate(
            flops=10 * count * rows * rows * wide, bytes_accessed=2 * rows * wide, transcendentals=0
        ),
        name="blocks_" + "_".join(str(d[0] if isinstance(d, tuple) else d) for d in distances),
    )(table, *arrays)


def join_kernel(table_ref, own_ref, other_ref, *refs, width):
    key_ref, value_ref, sink_key_ref, sink_value_ref = refs[-4:]
    rows = own_ref.shape[1]
    odd = jnp.full(own_ref.shape, table_ref[table_ref.shape[0] - 1] & 1, jnp.int32) == 1
    total = own_ref[...] + jnp.where(odd, 0.0, other_ref[:, rows:].astype(jnp.float32))
    turned = (total + sum_of(refs[:4])).T
    key_ref[...] = turned[:, :width]
    value_ref[...] = turned[:, width:]
    turned = sum_of(refs[4:-4]).T
    sink_key_ref[...] = turned[:, :width]
    sink_value_ref[...] = turned[:, width:]


def on_device(
    queries, keys, values, outputs, out_grad, lse, sink_keys, sink_values, window_len, sink_live
):
    rows = queries.shape[0]
    heads = lse.shape[0]
    width = keys.shape[1]
    sinks = sink_keys.shape[0]
    wide = heads * width
    shape = jax.ShapeDtypeStruct
    device = lax.axis_index(AXES).astype(jnp.int32).reshape(1)
    own_pair = jnp.concatenate([keys, values], axis=1)
    own_pair = pl.pallas_call(
        mark_kernel,
        out_shape=shape(own_pair.shape, LOW),
        in_specs=[ANY],
        out_specs=ANY,
        input_output_aliases={0: 0},
        compiler_params=pltpu.CompilerParams(vmem_limit_bytes=1024 * 1024),
        cost_estimate=pl.CostEstimate(flops=2 * 10**10, bytes_accessed=1, transcendentals=0),
        name="mark",
    )(own_pair)
    even = {d: rotated(own_pair, d) for d in (4, 2)}

    table, turned, row_terms, dquery, sink_grad, own_held = pl.pallas_call(
        functools.partial(sink_kernel, heads=heads, width=width, scale=width**-0.5),
        out_shape=(
            shape((heads + 1,), jnp.int32),
            shape((2 * wide, rows), LOW),
            shape((2 * heads, rows), jnp.float32),
            shape((wide, rows), jnp.float32),
            shape((2 * width, sinks), jnp.float32),
            shape((rows, 2 * width), LOW),
        ),
        in_specs=[SMEM] * 3 + [VMEM] * 8,
        out_specs=(SMEM,) + (VMEM,) * 5,
        compiler_params=pltpu.CompilerParams(vmem_limit_bytes=VMEM_BYTES),
        cost_estimate=pl.CostEstimate(flops=10**10, bytes_accessed=10**6, transcendentals=0),
        name="sink_keys_part",
    )(window_len, sink_live, device, keys, values, queries, out_grad, outputs, lse, sink_keys, sink_values)

    even.update({d: rotated(own_held, d) for d in (8, 6)})
    rounds = exchange_rounds()

    def sink_terms():
        return [sink_grad] + ([swapped(sink_grad, (rounds.pop(0),))] if rounds else [])

    terms = sink_terms()
    near, sink_grad = pl.pallas_call(
        near_kernel,
        out_shape=(shape((2 * rows, 2 * width), LOW), shape(sink_grad.shape, jnp.float32)),
        in_specs=[VMEM] * (2 + len(terms)),
        out_specs=(VMEM,) * 2,
        compiler_params=pltpu.CompilerParams(vmem_limit_bytes=VMEM_BYTES),
        name="near_blocks",
    )(even[2], even[4], *terms)
    partner = ((AXES[-1], 1),)
    near_odd = swapped(near, partner)
    while len(rounds) > 4:
        sink_grad = sum(sink_terms())
    terms = sink_terms()

    shared = (table, turned, row_terms)
    parts = [dquery]
    full = jnp.float32
    near_pair, far_pair = ((1, 3), (3, 5)), ((5, 7), (7, 1))
    part, grad_2, grad_4 = block_call([(2,), (4,)], [even[2], even[4]], shared, near, kind=full)
    parts.append(part)

    far, sink_grad = pl.pallas_call(
        far_kernel,
        out_shape=(shape((2 * rows, 2 * width), LOW), shape(sink_grad.shape, jnp.float32)),
        in_specs=[SMEM] + [VMEM] * 3 + [ANY] + [VMEM] * len(terms),
        out_specs=(VMEM,) * 2,
        compiler_params=pltpu.CompilerParams(vmem_limit_bytes=VMEM_BYTES),
        name="far_blocks",
    )(table, own_held, even[6], even[8], part, *terms)
    terms = sink_terms()
    far_odd = swapped(far, partner)

    part, near_mine = block_call([near_pair], [near_odd], shared, far, joined=True)
    parts.append(part)
    near_other = swapped(near_mine, partner)

    part, far_mine = block_call([far_pair], [far_odd], shared, part, joined=True)
    parts.append(part)
    far_other = swapped(far_mine, partner)

    def fold(first, second, other, after, near):
        return pl.pallas_call(
            functools.partial(fold_kernel, near=near),
            out_shape=(shape(first.shape, LOW),) * 2 + (shape(sink_grad.shape, jnp.float32),),
            in_specs=[SMEM] + [VMEM] * 3 + [ANY] + [VMEM] * len(terms),
            out_specs=(VMEM,) * 3,
            compiler_params=pltpu.CompilerParams(vmem_limit_bytes=VMEM_BYTES),
            name="fold",
        )(table, first, second, other, after, *terms)

    grad_2, grad_4, sink_grad = fold(grad_2, grad_4, near_other, far_mine, True)
    terms = sink_terms()
    backs = [rotated(grad_2, -2), rotated(grad_4, -4)]
    part, grad_6, grad_8 = block_call([(6,), (8,)], [even[6], even[8]], shared, grad_4, kind=full)
    parts.append(part)
    grad_6, grad_8, sink_grad = fold(grad_6, grad_8, far_other, part, False)
    terms = sink_terms()
    backs += [rotated(grad_6, -6), rotated(grad_8, -8)]
    dquery, own_grad = block_call(
        [(0,)], [own_held], shared, grad_8, parts=parts, kind=full, last=True,
        groups=((2, 4), near_pair, far_pair, (6, 8)),
    )
    key_grad, value_grad, sink_key_grad, sink_value_grad = pl.pallas_call(
        functools.partial(join_kernel, width=width),
        out_shape=(shape((rows, width), jnp.float32),) * 2 + (shape((sinks, width), jnp.float32),) * 2,
        in_specs=[SMEM] + [VMEM] * (6 + len(terms)),
        out_specs=(VMEM,) * 4,
        compiler_params=pltpu.CompilerParams(vmem_limit_bytes=VMEM_BYTES),
        name="join",
    )(table, own_grad, far_other, *backs, *terms)
    return (dquery, key_grad, value_grad, sink_key_grad, sink_value_grad)


def solution(mesh):
    split = P(AXES, None)
    return jax.shard_map(
        on_device,
        mesh=mesh,
        in_specs=(split,) * 5 + (P(None, AXES),) + (P(),) * 4,
        out_specs=(split,) * 3 + (P(),) * 2,
        check_vma=False,
    )
```

```python
import functools
import math

import jax
import jax.numpy as jnp
from jax import lax
from jax.experimental import pallas as pl
from jax.experimental.pallas import tpu as pltpu
from jax.sharding import PartitionSpec as P

WIN = 2048
AXES = ("seqhi", "seqlo")
LOG2E = math.log2(math.e)
NN = (((1,), (0,)), ((), ()))
NT = (((1,), (1,)), ((), ()))
VMEM_BYTES = 22 * 1024 * 1024
UNROLL = 4
AHEAD = 2
LOW = jnp.bfloat16
VMEM = pl.BlockSpec(memory_space=pltpu.VMEM)
SMEM = pl.BlockSpec(memory_space=pltpu.SMEM)
HBM = pl.BlockSpec(memory_space=pltpu.HBM)
ANY = pl.BlockSpec(memory_space=pl.ANY)


def dot(left, right, dims=NN):
    return lax.dot_general(left, right, dims, preferred_element_type=jnp.float32)


def rotated(block, distance):
    count = lax.axis_size(AXES)
    return lax.ppermute(block, AXES, [(i, (i + distance) % count) for i in range(count)])


def swapped(block, move):
    flips = dict.fromkeys(AXES, 0)
    for axis, step in move:
        flips[axis] ^= step
    sizes = [lax.axis_size(axis) for axis in AXES]
    route = []
    for i in range(sizes[0] * sizes[1]):
        high, low = divmod(i, sizes[1])
        route.append((i, (high ^ flips[AXES[0]]) * sizes[1] + (low ^ flips[AXES[1]])))
    return lax.ppermute(block, AXES, route)


def exchange_rounds():
    bits = {axis: [1 << bit for bit in range(lax.axis_size(axis).bit_length() - 1)] for axis in AXES}
    first, rest = bits[AXES[0]][:1], bits[AXES[0]][1:]
    low, high = bits[AXES[1]][:1], bits[AXES[1]][1:]
    order = [(AXES[0], first), (AXES[1], high), (AXES[1], low), (AXES[0], rest)]
    return [(axis, step) for axis, steps in order for step in steps]


def span(index, size):
    return pl.ds(pl.multiple_of(index * size, size), size)


def sink_kernel(
    window_ref, live_ref, device_ref, key_ref, value_ref, query_ref, grad_ref, out_ref, lse_in, sink_key_ref, sink_value_ref,
    table_ref, turned_ref, row_ref, dquery_ref, sink_grad_ref, own_ref,
    *, heads, width, scale,
):
    rows = query_ref.shape[0]
    sinks = sink_key_ref.shape[0]
    sink_grad_ref[...] = jnp.zeros_like(sink_grad_ref)
    for head in range(heads):
        table_ref[head] = window_ref[head]
    table_ref[heads] = device_ref[0]
    own_ref[:, :width] = key_ref[...]
    own_ref[:, width:] = value_ref[...]
    row_ref[:heads, :] = lse_in[...] * LOG2E
    key, value = sink_key_ref[...], sink_value_ref[...]
    key_t = key.T

    at = lax.broadcasted_iota(jnp.int32, (sinks, rows), 0)

    def some_heads(step, carry):
        heads_here = [UNROLL * step + part for part in range(UNROLL)]
        query_t, grad_t, keep, delta = [], [], [], []
        for head in heads_here:
            strip = span(head, width)
            query_t.append(query_ref[:, strip].T)
            grad_t.append(grad_ref[:, strip].T)
            turned_ref[strip, :] = query_t[-1]
            turned_ref[span(heads + head, width), :] = grad_t[-1]
            product = grad_t[-1].astype(jnp.float32) * out_ref[:, strip].T.astype(jnp.float32)
            delta.append(jnp.sum(product, axis=0, keepdims=True))
            row_ref[pl.ds(heads + head, 1), :] = delta[-1]
            keep.append(at < live_ref[head])
        lse = jnp.concatenate([lse_in[pl.ds(head, 1), :] for head in heads_here], axis=1) * LOG2E
        query_t, grad_t, keep, delta = (jnp.concatenate(x, axis=1) for x in (query_t, grad_t, keep, delta))
        probs = jnp.exp2(dot(key, query_t) * (scale * LOG2E) - lse)
        probs = jnp.where(keep, probs, 0.0)
        dscores = (probs * (dot(value, grad_t) - delta)).astype(LOW)
        sink_grad_ref[:width, :] += dot(query_t, dscores, NT) * scale
        sink_grad_ref[width:, :] += dot(grad_t, probs.astype(LOW), NT)
        dquery = dot(key_t, dscores)
        for part, head in enumerate(heads_here):
            dquery_ref[span(head, width), :] = dquery[:, part * rows : (part + 1) * rows]
        return carry

    lax.fori_loop(0, heads // UNROLL, some_heads, 0)


def sum_of(refs):
    total = refs[0][...].astype(jnp.float32)
    for ref in refs[1:]:
        total = total + ref[...].astype(jnp.float32)
    return total


def mark_kernel(block_ref, same_ref):
    pass


def fold_kernel(table_ref, first_ref, second_ref, other_ref, after_ref, *refs, near):
    first_out, second_out, sum_ref = refs[-3:]
    rows = first_ref.shape[1]
    first_out[...] = (first_ref[...] + other_ref[:, :rows].astype(jnp.float32)).astype(LOW)
    other = other_ref[:, rows:].astype(jnp.float32)
    if not near:
        odd = jnp.full(other.shape, table_ref[table_ref.shape[0] - 1] & 1, jnp.int32) == 1
        other = jnp.where(odd, other, 0.0)
    second_out[...] = (second_ref[...] + other).astype(LOW)
    sum_ref[...] = sum_of(refs[:-3])


def near_kernel(two_ref, four_ref, *refs):
    near_ref, sum_ref = refs[-2:]
    rows = two_ref.shape[0]
    near_ref[:rows, :] = two_ref[...]
    near_ref[rows:, :] = four_ref[...]
    sum_ref[...] = sum_of(refs[:-2])


def far_kernel(table_ref, own_ref, six_ref, eight_ref, after_ref, *refs):
    far_ref, sum_ref = refs[-2:]
    rows = own_ref.shape[0]
    odd = jnp.full(own_ref.shape, table_ref[table_ref.shape[0] - 1] & 1, jnp.int32) == 1
    far_ref[:rows, :] = six_ref[...]
    far_ref[rows:, :] = jnp.where(odd, eight_ref[...], own_ref[...])
    sum_ref[...] = sum_of(refs[:-2])


def local(distances, device):
    return [
        jnp.where(device & 1 == 1, distance[1], distance[0]) if isinstance(distance, tuple) else distance
        for distance in distances
    ]


def block_kernel(*refs, layout, groups, heads, width, scale):
    refs = list(refs)

    def take(count):
        taken = refs[:count]
        del refs[:count]
        return taken

    pairs, joined, last = layout
    table_ref, turned_ref, row_ref = take(3)
    device = table_ref[heads]
    distances = local([distance for pair in pairs for distance in pair], device)
    pair_refs = take(len(pairs))
    part_refs = take(1 + len(groups)) if last else []
    take(1)
    dquery_ref = take(1)[0]
    out_refs = take(1 if joined else len(distances))
    items_ref, pair_ref, key_t_ref, sum_ref = take(4)
    low_refs = take(2 * AHEAD + 4)
    total_ref, total_sems = take(2) if last else (None, None)
    rows = pair_ref.shape[1]
    unroll = UNROLL if last else 2 * UNROLL

    slot = 0
    for ref, members in zip(pair_refs, pairs):
        for place in range(len(members)):
            block = ref[place * rows : (place + 1) * rows, :]
            pair_ref[slot] = block
            key_t_ref[slot] = block[:, :width].T
            slot += 1
    sum_ref[...] = jnp.zeros_like(sum_ref)
    for ref in low_refs:
        ref[...] = jnp.zeros_like(ref)

    def needed(head, distance):
        return (table_ref[head] - distance * rows > 1 - rows) & (device >= distance)

    def list_head(head, found):
        before = found
        for slot, distance in enumerate(distances):
            items_ref[0, found] = slot
            items_ref[1, found] = head
            items_ref[2, found] = table_ref[head] - distance * rows
            items_ref[3, found] = (found == before).astype(jnp.int32)
            found = found + needed(head, distance).astype(jnp.int32)
        return found

    found = lax.fori_loop(0, heads, list_head, 0)
    steps = lax.div(found + unroll - 1, unroll)

    def pad_item(index, carry):
        items_ref[0, index] = 0
        items_ref[1, index] = 0
        items_ref[2, index] = -rows
        items_ref[3, index] = 0
        return carry

    lax.fori_loop(found, steps * unroll, pad_item, 0)

    def produce(index, probs_ref, dscores_ref):
        slot, head, left = items_ref[0, index], items_ref[1, index], items_ref[2, index]
        strip = span(head, width)
        scores = dot(pair_ref[slot, :, :width], turned_ref[strip, :])
        probs = jnp.exp2(scores * (scale * LOG2E) - row_ref[pl.ds(head, 1), :])
        key_at = lax.broadcasted_iota(jnp.int32, (rows, 1), 0)
        query_at = lax.broadcasted_iota(jnp.int32, (1, rows), 1)
        keep = query_at - left < key_at
        if last:
            keep = keep & (key_at <= query_at)
        probs = jnp.where(keep, probs, 0.0)
        dprobs = dot(pair_ref[slot, :, width:], turned_ref[span(heads + head, width), :])
        probs_ref[...] = probs.astype(LOW)
        dscores_ref[...] = (probs * (dprobs - row_ref[pl.ds(heads + head, 1), :])).astype(LOW)

    def consume(index, probs_ref, dscores_ref):
        slot, head = items_ref[0, index], items_ref[1, index]
        strip = span(head, width)
        dscores = dscores_ref[...]
        sum_ref[slot, width:, :] += dot(turned_ref[span(heads + head, width), :], probs_ref[...], NT)
        sum_ref[slot, :width, :] += dot(turned_ref[strip, :], dscores, NT)
        dquery = dot(key_t_ref[slot], dscores)
        if last:
            dquery = dquery + part_refs[0][strip, :]
            for ref, group in zip(part_refs[1:], groups):
                touched = functools.reduce(jnp.logical_or, [needed(head, distance) for distance in local(group, device)])
                dquery = dquery + jnp.where(touched, ref[strip, :], 0.0)
            total_ref[:, strip] = dquery.T * scale
        else:
            dquery_ref[strip, :] = dquery + jnp.where(items_ref[3, index] == 1, 0.0, dquery_ref[strip, :])

    buffers = [low_refs[2 * at : 2 * at + 2] for at in range(AHEAD + 2)]

    def total_copy(step):
        lanes = span(step, UNROLL * width)
        return pltpu.make_async_copy(total_ref.at[:, lanes], dquery_ref.at[:, lanes], total_sems.at[step])

    def some_items(step, carry):
        for part in range(unroll):
            index = step * unroll + part
            produce(index, *buffers[part % len(buffers)])
            consume(jnp.maximum(index - AHEAD, 0), *buffers[(part - AHEAD) % len(buffers)])
        if last:
            pl.when(step > 0)(lambda: total_copy(step - 1).start())
        return carry

    lax.fori_loop(0, steps, some_items, 0)

    @pl.when(found > 0)
    def _():
        for at in range(unroll - AHEAD, unroll):
            consume((steps - 1) * unroll + at, *buffers[at % len(buffers)])

    if last:
        total_copy(heads // UNROLL - 1).start()
    for slot in range(len(distances)):
        grads = (sum_ref[slot, :width, :] * scale, sum_ref[slot, width:, :])
        for half, grad in enumerate(grads):
            strip = slice(half * width, (half + 1) * width)
            if joined:
                out_refs[0][strip, slot * rows : (slot + 1) * rows] = grad.astype(out_refs[0].dtype)
            else:
                out_refs[slot][strip, :] = grad.astype(out_refs[slot].dtype)
    if last:
        for step in range(heads // UNROLL):
            total_copy(step).wait()


def block_call(pairs, pair_arrays, shared, after, parts=(), groups=(), last=False, kind=LOW, joined=False):
    table, turned, row_terms = shared
    wide, rows = turned.shape[0] // 2, turned.shape[1]
    heads = row_terms.shape[0] // 2
    width = wide // heads
    distances = [distance for pair in pairs for distance in pair]
    count = len(distances)
    shape = jax.ShapeDtypeStruct
    outs = [shape((rows, wide) if last else (wide, rows), jnp.float32)]
    outs += [shape((2 * width, count * rows), kind)] if joined else [shape((2 * width, rows), kind)] * count
    arrays = [turned, row_terms, *pair_arrays, *parts, after]
    layout = (pairs, joined, last)
    return pl.pallas_call(
        functools.partial(
            block_kernel, layout=layout, groups=groups, heads=heads, width=width, scale=width**-0.5
        ),
        out_shape=outs,
        in_specs=[SMEM] + [VMEM] * (len(arrays) - 1) + [ANY],
        out_specs=[HBM if last else VMEM] + [VMEM] * (len(outs) - 1),
        scratch_shapes=[
            pltpu.SMEM((4, count * heads + 2 * UNROLL), jnp.int32),
            pltpu.VMEM((count, rows, 2 * width), LOW),
            pltpu.VMEM((count, width, rows), LOW),
            pltpu.VMEM((count, 2 * width, rows), jnp.float32),
        ]
        + [pltpu.VMEM((rows, rows), LOW)] * (2 * AHEAD + 4)
        + ([pltpu.VMEM((rows, wide), jnp.float32), pltpu.SemaphoreType.DMA((heads // UNROLL,))] if last else []),
        compiler_params=pltpu.CompilerParams(vmem_limit_bytes=VMEM_BYTES),
        cost_estimate=pl.CostEstimate(
            flops=10 * count * rows * rows * wide, bytes_accessed=2 * rows * wide, transcendentals=0
        ),
        name="blocks_" + "_".join(str(d[0] if isinstance(d, tuple) else d) for d in distances),
    )(table, *arrays)


def join_kernel(table_ref, own_ref, other_ref, *refs, width):
    key_ref, value_ref, sink_key_ref, sink_value_ref = refs[-4:]
    rows = own_ref.shape[1]
    odd = jnp.full(own_ref.shape, table_ref[table_ref.shape[0] - 1] & 1, jnp.int32) == 1
    total = own_ref[...] + jnp.where(odd, 0.0, other_ref[:, rows:].astype(jnp.float32))
    turned = (total + sum_of(refs[:4])).T
    key_ref[...] = turned[:, :width]
    value_ref[...] = turned[:, width:]
    turned = sum_of(refs[4:-4]).T
    sink_key_ref[...] = turned[:, :width]
    sink_value_ref[...] = turned[:, width:]


def on_device(
    queries, keys, values, outputs, out_grad, lse, sink_keys, sink_values, window_len, sink_live
):
    rows = queries.shape[0]
    heads = lse.shape[0]
    width = keys.shape[1]
    sinks = sink_keys.shape[0]
    wide = heads * width
    shape = jax.ShapeDtypeStruct
    device = lax.axis_index(AXES).astype(jnp.int32).reshape(1)
    own_pair = jnp.concatenate([keys, values], axis=1)
    own_pair = pl.pallas_call(
        mark_kernel,
        out_shape=shape(own_pair.shape, LOW),
        in_specs=[ANY],
        out_specs=ANY,
        input_output_aliases={0: 0},
        compiler_params=pltpu.CompilerParams(vmem_limit_bytes=1024 * 1024),
        cost_estimate=pl.CostEstimate(flops=2 * 10**10, bytes_accessed=1, transcendentals=0),
        name="mark",
    )(own_pair)
    even = {d: rotated(own_pair, d) for d in (4, 2)}

    table, turned, row_terms, dquery, sink_grad, own_held = pl.pallas_call(
        functools.partial(sink_kernel, heads=heads, width=width, scale=width**-0.5),
        out_shape=(
            shape((heads + 1,), jnp.int32),
            shape((2 * wide, rows), LOW),
            shape((2 * heads, rows), jnp.float32),
            shape((wide, rows), jnp.float32),
            shape((2 * width, sinks), jnp.float32),
            shape((rows, 2 * width), LOW),
        ),
        in_specs=[SMEM] * 3 + [VMEM] * 8,
        out_specs=(SMEM,) + (VMEM,) * 5,
        compiler_params=pltpu.CompilerParams(vmem_limit_bytes=VMEM_BYTES),
        cost_estimate=pl.CostEstimate(flops=10**10, bytes_accessed=10**6, transcendentals=0),
        name="sink_keys_part",
    )(window_len, sink_live, device, keys, values, queries, out_grad, outputs, lse, sink_keys, sink_values)

    even.update({d: rotated(own_held, d) for d in (8, 6)})
    rounds = exchange_rounds()

    def sink_terms():
        return [sink_grad] + ([swapped(sink_grad, (rounds.pop(0),))] if rounds else [])

    terms = sink_terms()
    near, sink_grad = pl.pallas_call(
        near_kernel,
        out_shape=(shape((2 * rows, 2 * width), LOW), shape(sink_grad.shape, jnp.float32)),
        in_specs=[VMEM] * (2 + len(terms)),
        out_specs=(VMEM,) * 2,
        compiler_params=pltpu.CompilerParams(vmem_limit_bytes=VMEM_BYTES),
        name="near_blocks",
    )(even[2], even[4], *terms)
    partner = ((AXES[-1], 1),)
    near_odd = swapped(near, partner)
    while len(rounds) > 4:
        sink_grad = sum(sink_terms())
    terms = sink_terms()

    shared = (table, turned, row_terms)
    parts = [dquery]
    full = jnp.float32
    near_pair, far_pair = ((1, 3), (3, 5)), ((5, 7), (7, 1))
    part, grad_2, grad_4 = block_call([(2,), (4,)], [even[2], even[4]], shared, near, kind=full)
    parts.append(part)

    far, sink_grad = pl.pallas_call(
        far_kernel,
        out_shape=(shape((2 * rows, 2 * width), LOW), shape(sink_grad.shape, jnp.float32)),
        in_specs=[SMEM] + [VMEM] * 3 + [ANY] + [VMEM] * len(terms),
        out_specs=(VMEM,) * 2,
        compiler_params=pltpu.CompilerParams(vmem_limit_bytes=VMEM_BYTES),
        name="far_blocks",
    )(table, own_held, even[6], even[8], part, *terms)
    terms = sink_terms()
    far_odd = swapped(far, partner)

    part, near_mine = block_call([near_pair], [near_odd], shared, far, joined=True)
    parts.append(part)
    near_other = swapped(near_mine, partner)

    part, far_mine = block_call([far_pair], [far_odd], shared, part, joined=True)
    parts.append(part)
    far_other = swapped(far_mine, partner)

    def fold(first, second, other, after, near):
        return pl.pallas_call(
            functools.partial(fold_kernel, near=near),
            out_shape=(shape(first.shape, LOW),) * 2 + (shape(sink_grad.shape, jnp.float32),),
            in_specs=[SMEM] + [VMEM] * 3 + [ANY] + [VMEM] * len(terms),
            out_specs=(VMEM,) * 3,
            compiler_params=pltpu.CompilerParams(vmem_limit_bytes=VMEM_BYTES),
            name="fold",
        )(table, first, second, other, after, *terms)

    grad_2, grad_4, sink_grad = fold(grad_2, grad_4, near_other, far_mine, True)
    terms = sink_terms()
    backs = [rotated(grad_2, -2), rotated(grad_4, -4)]
    part, grad_6, grad_8 = block_call([(6,), (8,)], [even[6], even[8]], shared, grad_4, kind=full)
    parts.append(part)
    grad_6, grad_8, sink_grad = fold(grad_6, grad_8, far_other, part, False)
    terms = sink_terms()
    backs += [rotated(grad_6, -6), rotated(grad_8, -8)]
    dquery, own_grad = block_call(
        [(0,)], [own_held], shared, grad_8, parts=parts, kind=full, last=True,
        groups=((2, 4), near_pair, far_pair, (6, 8)),
    )
    key_grad, value_grad, sink_key_grad, sink_value_grad = pl.pallas_call(
        functools.partial(join_kernel, width=width),
        out_shape=(shape((rows, width), jnp.float32),) * 2 + (shape((sinks, width), jnp.float32),) * 2,
        in_specs=[SMEM] + [VMEM] * (6 + len(terms)),
        out_specs=(VMEM,) * 4,
        compiler_params=pltpu.CompilerParams(vmem_limit_bytes=VMEM_BYTES),
        name="join",
    )(table, own_grad, far_other, *backs, *terms)
    return (dquery, key_grad, value_grad, sink_key_grad, sink_value_grad)


def solution(mesh):
    split = P(AXES, None)
    return jax.shard_map(
        on_device,
        mesh=mesh,
        in_specs=(split,) * 5 + (P(None, AXES),) + (P(),) * 4,
        out_specs=(split,) * 3 + (P(),) * 2,
        check_vma=False,
    )
```

```python
import functools
import math

import jax
import jax.numpy as jnp
from jax import lax
from jax.experimental import pallas as pl
from jax.experimental.pallas import tpu as pltpu
from jax.sharding import PartitionSpec as P

WIN = 2048
AXES = ("seqhi", "seqlo")
LOG2E = math.log2(math.e)
NN = (((1,), (0,)), ((), ()))
NT = (((1,), (1,)), ((), ()))
VMEM_BYTES = 22 * 1024 * 1024
UNROLL = 4
AHEAD = 2
LOW = jnp.bfloat16
VMEM = pl.BlockSpec(memory_space=pltpu.VMEM)
SMEM = pl.BlockSpec(memory_space=pltpu.SMEM)
HBM = pl.BlockSpec(memory_space=pltpu.HBM)
ANY = pl.BlockSpec(memory_space=pl.ANY)


def dot(left, right, dims=NN):
    return lax.dot_general(left, right, dims, preferred_element_type=jnp.float32)


def rotated(block, distance):
    count = lax.axis_size(AXES)
    return lax.ppermute(block, AXES, [(i, (i + distance) % count) for i in range(count)])


def swapped(block, move):
    flips = dict.fromkeys(AXES, 0)
    for axis, step in move:
        flips[axis] ^= step
    sizes = [lax.axis_size(axis) for axis in AXES]
    route = []
    for i in range(sizes[0] * sizes[1]):
        high, low = divmod(i, sizes[1])
        route.append((i, (high ^ flips[AXES[0]]) * sizes[1] + (low ^ flips[AXES[1]])))
    return lax.ppermute(block, AXES, route)


def exchange_rounds():
    bits = {axis: [1 << bit for bit in range(lax.axis_size(axis).bit_length() - 1)] for axis in AXES}
    first, rest = bits[AXES[0]][:1], bits[AXES[0]][1:]
    low, high = bits[AXES[1]][:1], bits[AXES[1]][1:]
    order = [(AXES[0], first), (AXES[1], high), (AXES[0], rest), (AXES[1], low)]
    return [(axis, step) for axis, steps in order for step in steps]


def span(index, size):
    return pl.ds(pl.multiple_of(index * size, size), size)


def sink_kernel(
    window_ref, live_ref, device_ref, key_ref, value_ref, query_ref, grad_ref, out_ref, lse_in, sink_key_ref, sink_value_ref,
    table_ref, turned_ref, row_ref, dquery_ref, sink_grad_ref, own_ref,
    *, heads, width, scale,
):
    rows = query_ref.shape[0]
    sinks = sink_key_ref.shape[0]
    sink_grad_ref[...] = jnp.zeros_like(sink_grad_ref)
    for head in range(heads):
        table_ref[head] = window_ref[head]
    table_ref[heads] = device_ref[0]
    own_ref[:, :width] = key_ref[...]
    own_ref[:, width:] = value_ref[...]
    row_ref[:heads, :] = lse_in[...] * LOG2E
    key, value = sink_key_ref[...], sink_value_ref[...]
    key_t = key.T

    at = lax.broadcasted_iota(jnp.int32, (sinks, rows), 0)

    def some_heads(step, carry):
        heads_here = [UNROLL * step + part for part in range(UNROLL)]
        query_t, grad_t, keep, delta = [], [], [], []
        for head in heads_here:
            strip = span(head, width)
            query_t.append(query_ref[:, strip].T)
            grad_t.append(grad_ref[:, strip].T)
            turned_ref[strip, :] = query_t[-1]
            turned_ref[span(heads + head, width), :] = grad_t[-1]
            product = grad_t[-1].astype(jnp.float32) * out_ref[:, strip].T.astype(jnp.float32)
            delta.append(jnp.sum(product, axis=0, keepdims=True))
            row_ref[pl.ds(heads + head, 1), :] = delta[-1]
            keep.append(at < live_ref[head])
        lse = jnp.concatenate([lse_in[pl.ds(head, 1), :] for head in heads_here], axis=1) * LOG2E
        query_t, grad_t, keep, delta = (jnp.concatenate(x, axis=1) for x in (query_t, grad_t, keep, delta))
        probs = jnp.exp2(dot(key, query_t) * (scale * LOG2E) - lse)
        probs = jnp.where(keep, probs, 0.0)
        dscores = (probs * (dot(value, grad_t) - delta)).astype(LOW)
        sink_grad_ref[:width, :] += dot(query_t, dscores, NT) * scale
        sink_grad_ref[width:, :] += dot(grad_t, probs.astype(LOW), NT)
        dquery = dot(key_t, dscores)
        for part, head in enumerate(heads_here):
            dquery_ref[span(head, width), :] = dquery[:, part * rows : (part + 1) * rows]
        return carry

    lax.fori_loop(0, heads // UNROLL, some_heads, 0)


def sum_of(refs):
    total = refs[0][...].astype(jnp.float32)
    for ref in refs[1:]:
        total = total + ref[...].astype(jnp.float32)
    return total


def mark_kernel(block_ref, same_ref):
    pass


def fold_kernel(table_ref, first_ref, second_ref, other_ref, after_ref, *refs, near):
    first_out, second_out, sum_ref = refs[-3:]
    rows = first_ref.shape[1]
    first_out[...] = (first_ref[...] + other_ref[:, :rows].astype(jnp.float32)).astype(LOW)
    other = other_ref[:, rows:].astype(jnp.float32)
    if not near:
        odd = jnp.full(other.shape, table_ref[table_ref.shape[0] - 1] & 1, jnp.int32) == 1
        other = jnp.where(odd, other, 0.0)
    second_out[...] = (second_ref[...] + other).astype(LOW)
    sum_ref[...] = sum_of(refs[:-3]).astype(sum_ref.dtype)


def near_kernel(two_ref, four_ref, *refs):
    near_ref, sum_ref = refs[-2:]
    rows = two_ref.shape[0]
    near_ref[:rows, :] = two_ref[...]
    near_ref[rows:, :] = four_ref[...]
    sum_ref[...] = sum_of(refs[:-2])


def far_kernel(table_ref, own_ref, six_ref, eight_ref, after_ref, *refs):
    far_ref, sum_ref = refs[-2:]
    rows = own_ref.shape[0]
    odd = jnp.full(own_ref.shape, table_ref[table_ref.shape[0] - 1] & 1, jnp.int32) == 1
    far_ref[:rows, :] = six_ref[...]
    far_ref[rows:, :] = jnp.where(odd, eight_ref[...], own_ref[...])
    sum_ref[...] = sum_of(refs[:-2])


def local(distances, device):
    return [
        jnp.where(device & 1 == 1, distance[1], distance[0]) if isinstance(distance, tuple) else distance
        for distance in distances
    ]


def block_kernel(*refs, layout, groups, heads, width, scale):
    refs = list(refs)

    def take(count):
        taken = refs[:count]
        del refs[:count]
        return taken

    pairs, joined, last = layout
    table_ref, turned_ref, row_ref = take(3)
    device = table_ref[heads]
    distances = local([distance for pair in pairs for distance in pair], device)
    pair_refs = take(len(pairs))
    part_refs = take(1 + len(groups)) if last else []
    other_refs = take(1) if last else []
    take(1)
    dquery_ref = take(1)[0]
    out_refs = take(1 if joined else len(distances))
    items_ref, pair_ref, key_t_ref, sum_ref = take(4)
    low_refs = take(2 * AHEAD + 4)
    total_ref, total_sems = take(2) if last else (None, None)
    rows = pair_ref.shape[1]
    unroll = 2 * UNROLL

    slot = 0
    for ref, members in zip(pair_refs, pairs):
        for place in range(len(members)):
            block = ref[place * rows : (place + 1) * rows, :]
            pair_ref[slot] = block
            key_t_ref[slot] = block[:, :width].T
            slot += 1
    sum_ref[...] = jnp.zeros_like(sum_ref)
    for ref in low_refs[4:]:
        ref[...] = jnp.zeros_like(ref)

    def needed(head, distance):
        return (table_ref[head] - distance * rows > 1 - rows) & (device >= distance)

    def list_head(head, found):
        before = found
        for slot, distance in enumerate(distances):
            items_ref[0, found] = slot
            items_ref[1, found] = head
            items_ref[2, found] = table_ref[head] - distance * rows
            items_ref[3, found] = (found == before).astype(jnp.int32)
            found = found + needed(head, distance).astype(jnp.int32)
        return found

    found = lax.fori_loop(0, heads, list_head, 0, unroll=UNROLL)
    padded = lax.div(found + UNROLL - 1, UNROLL) * UNROLL
    steps = lax.div(padded, unroll)

    def pad_item(index, carry):
        items_ref[0, index] = 0
        items_ref[1, index] = 0
        items_ref[2, index] = -rows
        items_ref[3, index] = 0
        return carry

    lax.fori_loop(found, padded, pad_item, 0)

    def produce(index, probs_ref, dscores_ref):
        slot, head, left = items_ref[0, index], items_ref[1, index], items_ref[2, index]
        strip = span(head, width)
        scores = dot(pair_ref[slot, :, :width], turned_ref[strip, :])
        probs = jnp.exp2(scores * (scale * LOG2E) - row_ref[pl.ds(head, 1), :])
        key_at = lax.broadcasted_iota(jnp.int32, (rows, 1), 0)
        query_at = lax.broadcasted_iota(jnp.int32, (1, rows), 1)
        keep = query_at - left < key_at
        if last:
            keep = keep & (key_at <= query_at)
        probs = jnp.where(keep, probs, 0.0)
        dprobs = dot(pair_ref[slot, :, width:], turned_ref[span(heads + head, width), :])
        probs_ref[...] = probs.astype(LOW)
        dscores_ref[...] = (probs * (dprobs - row_ref[pl.ds(heads + head, 1), :])).astype(LOW)

    def consume(index, probs_ref, dscores_ref):
        slot, head = items_ref[0, index], items_ref[1, index]
        strip = span(head, width)
        dscores = dscores_ref[...]
        sum_ref[slot, width:, :] += dot(turned_ref[span(heads + head, width), :], probs_ref[...], NT)
        sum_ref[slot, :width, :] += dot(turned_ref[strip, :], dscores, NT)
        dquery = dot(key_t_ref[slot], dscores)
        if last:
            dquery = dquery + part_refs[0][strip, :]
            for ref, group in zip(part_refs[1:], groups):
                touched = functools.reduce(jnp.logical_or, [needed(head, distance) for distance in local(group, device)])
                dquery = dquery + jnp.where(touched, ref[strip, :], 0.0)
            total_ref[:, strip] = dquery.T * scale
        else:
            dquery_ref[strip, :] = dquery + jnp.where(items_ref[3, index] == 1, 0.0, dquery_ref[strip, :])

    buffers = [low_refs[2 * at : 2 * at + 2] for at in range(AHEAD + 2)]

    def total_copy(step):
        lanes = span(step, UNROLL * width)
        return pltpu.make_async_copy(total_ref.at[:, lanes], dquery_ref.at[:, lanes], total_sems.at[step])

    def some_items(step, carry, count=unroll):
        for part in range(count):
            index = step * unroll + part
            produce(index, *buffers[part % len(buffers)])
            consume(jnp.maximum(index - AHEAD, 0), *buffers[(part - AHEAD) % len(buffers)])
        if last:
            total_copy(2 * step).start()
            pl.when(step > 0)(lambda: total_copy(2 * step - 1).start())
        return carry

    lax.fori_loop(0, steps, some_items, 0)
    if not last:

        @pl.when(padded > steps * unroll)
        def _():
            some_items(steps, 0, UNROLL)

    @pl.when(found > 0)
    def _():
        for at in range(UNROLL - AHEAD, UNROLL):
            consume(padded - UNROLL + at, *buffers[at % len(buffers)])

    if last:
        total_copy(heads // UNROLL - 1).start()
    for slot in range(len(distances)):
        grads = (sum_ref[slot, :width, :] * scale, sum_ref[slot, width:, :])
        for half, grad in enumerate(grads):
            strip = slice(half * width, (half + 1) * width)
            for ref in other_refs:
                other = ref[strip, rows:].astype(jnp.float32)
                grad = grad + jnp.where(jnp.full(other.shape, device & 1, jnp.int32) == 1, 0.0, other)
            if joined:
                out_refs[0][strip, slot * rows : (slot + 1) * rows] = grad.astype(out_refs[0].dtype)
            else:
                out_refs[slot][strip, :] = grad.astype(out_refs[slot].dtype)
    if last:
        for step in range(heads // UNROLL):
            total_copy(step).wait()


def block_call(pairs, pair_arrays, shared, after, parts=(), others=(), groups=(), last=False, kind=LOW, joined=False):
    table, turned, row_terms = shared
    wide, rows = turned.shape[0] // 2, turned.shape[1]
    heads = row_terms.shape[0] // 2
    width = wide // heads
    distances = [distance for pair in pairs for distance in pair]
    count = len(distances)
    shape = jax.ShapeDtypeStruct
    outs = [shape((rows, wide) if last else (wide, rows), jnp.float32)]
    outs += [shape((2 * width, count * rows), kind)] if joined else [shape((2 * width, rows), kind)] * count
    arrays = [turned, row_terms, *pair_arrays, *parts, *others, after]
    layout = (pairs, joined, last)
    return pl.pallas_call(
        functools.partial(
            block_kernel, layout=layout, groups=groups, heads=heads, width=width, scale=width**-0.5
        ),
        out_shape=outs,
        in_specs=[SMEM] + [VMEM] * (len(arrays) - 1) + [ANY],
        out_specs=[HBM if last else VMEM] + [VMEM] * (len(outs) - 1),
        scratch_shapes=[
            pltpu.SMEM((4, count * heads + 2 * UNROLL), jnp.int32),
            pltpu.VMEM((count, rows, 2 * width), LOW),
            pltpu.VMEM((count, width, rows), LOW),
            pltpu.VMEM((count, 2 * width, rows), jnp.float32),
        ]
        + [pltpu.VMEM((rows, rows), LOW)] * (2 * AHEAD + 4)
        + ([pltpu.VMEM((rows, wide), jnp.float32), pltpu.SemaphoreType.DMA((heads // UNROLL,))] if last else []),
        compiler_params=pltpu.CompilerParams(vmem_limit_bytes=VMEM_BYTES),
        cost_estimate=pl.CostEstimate(
            flops=10 * count * rows * rows * wide, bytes_accessed=2 * rows * wide, transcendentals=0
        ),
        name="blocks_" + "_".join(str(d[0] if isinstance(d, tuple) else d) for d in distances),
    )(table, *arrays)


def join_kernel(*refs, width):
    key_ref, value_ref, sink_key_ref, sink_value_ref = refs[-4:]
    turned = sum_of(refs[:5]).T
    key_ref[...] = turned[:, :width]
    value_ref[...] = turned[:, width:]
    turned = sum_of(refs[5:-4]).T
    sink_key_ref[...] = turned[:, :width]
    sink_value_ref[...] = turned[:, width:]


def on_device(
    queries, keys, values, outputs, out_grad, lse, sink_keys, sink_values, window_len, sink_live
):
    rows = queries.shape[0]
    heads = lse.shape[0]
    width = keys.shape[1]
    sinks = sink_keys.shape[0]
    wide = heads * width
    shape = jax.ShapeDtypeStruct
    device = lax.axis_index(AXES).astype(jnp.int32).reshape(1)
    own_pair = jnp.concatenate([keys, values], axis=1)
    own_pair = pl.pallas_call(
        mark_kernel,
        out_shape=shape(own_pair.shape, LOW),
        in_specs=[ANY],
        out_specs=ANY,
        input_output_aliases={0: 0},
        compiler_params=pltpu.CompilerParams(vmem_limit_bytes=1024 * 1024),
        cost_estimate=pl.CostEstimate(flops=2 * 10**10, bytes_accessed=1, transcendentals=0),
        name="mark",
    )(own_pair)
    even = {d: rotated(own_pair, d) for d in (4, 2)}

    table, turned, row_terms, dquery, sink_grad, own_held = pl.pallas_call(
        functools.partial(sink_kernel, heads=heads, width=width, scale=width**-0.5),
        out_shape=(
            shape((heads + 1,), jnp.int32),
            shape((2 * wide, rows), LOW),
            shape((2 * heads, rows), jnp.float32),
            shape((wide, rows), jnp.float32),
            shape((2 * width, sinks), jnp.float32),
            shape((rows, 2 * width), LOW),
        ),
        in_specs=[SMEM] * 3 + [VMEM] * 8,
        out_specs=(SMEM,) + (VMEM,) * 5,
        compiler_params=pltpu.CompilerParams(vmem_limit_bytes=VMEM_BYTES),
        cost_estimate=pl.CostEstimate(flops=10**10, bytes_accessed=10**6, transcendentals=0),
        name="sink_keys_part",
    )(window_len, sink_live, device, keys, values, queries, out_grad, outputs, lse, sink_keys, sink_values)

    even.update({d: rotated(own_held, d) for d in (8, 6)})
    rounds = exchange_rounds()

    def sink_terms():
        return [sink_grad] + ([swapped(sink_grad, (rounds.pop(0),))] if rounds else [])

    terms = sink_terms()
    near, sink_grad = pl.pallas_call(
        near_kernel,
        out_shape=(shape((2 * rows, 2 * width), LOW), shape(sink_grad.shape, jnp.float32)),
        in_specs=[VMEM] * (2 + len(terms)),
        out_specs=(VMEM,) * 2,
        compiler_params=pltpu.CompilerParams(vmem_limit_bytes=VMEM_BYTES),
        name="near_blocks",
    )(even[2], even[4], *terms)
    partner = ((AXES[-1], 1),)
    near_odd = swapped(near, partner)
    while len(rounds) > 4:
        sink_grad = sum(sink_terms())
    terms = sink_terms()

    shared = (table, turned, row_terms)
    parts = [dquery]
    full = jnp.float32
    near_pair, far_pair = ((1, 3), (3, 5)), ((5, 7), (7, 1))
    part, grad_2, grad_4 = block_call([(2,), (4,)], [even[2], even[4]], shared, near, kind=full)
    parts.append(part)

    far, sink_grad = pl.pallas_call(
        far_kernel,
        out_shape=(shape((2 * rows, 2 * width), LOW), shape(sink_grad.shape, jnp.float32)),
        in_specs=[SMEM] + [VMEM] * 3 + [ANY] + [VMEM] * len(terms),
        out_specs=(VMEM,) * 2,
        compiler_params=pltpu.CompilerParams(vmem_limit_bytes=VMEM_BYTES),
        name="far_blocks",
    )(table, own_held, even[6], even[8], part, *terms)
    terms = sink_terms()
    far_odd = swapped(far, partner)

    part, near_mine = block_call([near_pair], [near_odd], shared, far, joined=True)
    parts.append(part)
    near_other = swapped(near_mine, partner)

    part, far_mine = block_call([far_pair], [far_odd], shared, part, joined=True)
    parts.append(part)
    far_other = swapped(far_mine, partner)

    def fold(first, second, other, after, near):
        return pl.pallas_call(
            functools.partial(fold_kernel, near=near),
            out_shape=(shape(first.shape, LOW),) * 2 + (shape(sink_grad.shape, full if near else LOW),),
            in_specs=[SMEM] + [VMEM] * 3 + [ANY] + [VMEM] * len(terms),
            out_specs=(VMEM,) * 3,
            compiler_params=pltpu.CompilerParams(vmem_limit_bytes=VMEM_BYTES),
            name="fold",
        )(table, first, second, other, after, *terms)

    grad_2, grad_4, sink_grad = fold(grad_2, grad_4, near_other, far_mine, True)
    terms = sink_terms()
    backs = [rotated(grad_2, -2), rotated(grad_4, -4)]
    part, grad_6, grad_8 = block_call([(6,), (8,)], [even[6], even[8]], shared, grad_4, kind=full)
    parts.append(part)
    grad_6, grad_8, sink_grad = fold(grad_6, grad_8, far_other, part, False)
    terms = sink_terms()
    backs += [rotated(grad_6, -6), rotated(grad_8, -8)]
    dquery, own_grad = block_call(
        [(0,)], [own_held], shared, grad_8, parts=parts, others=(far_other,), kind=full, last=True,
        groups=((2, 4), near_pair, far_pair, (6, 8)),
    )
    key_grad, value_grad, sink_key_grad, sink_value_grad = pl.pallas_call(
        functools.partial(join_kernel, width=width),
        out_shape=(shape((rows, width), jnp.float32),) * 2 + (shape((sinks, width), jnp.float32),) * 2,
        in_specs=[VMEM] * (5 + len(terms)),
        out_specs=(VMEM,) * 4,
        compiler_params=pltpu.CompilerParams(vmem_limit_bytes=VMEM_BYTES),
        name="join",
    )(own_grad, *backs, *terms)
    return (dquery, key_grad, value_grad, sink_key_grad, sink_value_grad)


def solution(mesh):
    split = P(AXES, None)
    return jax.shard_map(
        on_device,
        mesh=mesh,
        in_specs=(split,) * 5 + (P(None, AXES),) + (P(),) * 4,
        out_specs=(split,) * 3 + (P(),) * 2,
        check_vma=False,
    )
```

```python
import functools
import math

import jax
import jax.numpy as jnp
from jax import lax
from jax.experimental import pallas as pl
from jax.experimental.pallas import tpu as pltpu
from jax.sharding import PartitionSpec as P

WIN = 2048
AXES = ("seqhi", "seqlo")
LOG2E = math.log2(math.e)
NN = (((1,), (0,)), ((), ()))
NT = (((1,), (1,)), ((), ()))
VMEM_BYTES = 22 * 1024 * 1024
UNROLL = 4
AHEAD = 2
LOW = jnp.bfloat16
VMEM = pl.BlockSpec(memory_space=pltpu.VMEM)
SMEM = pl.BlockSpec(memory_space=pltpu.SMEM)
HBM = pl.BlockSpec(memory_space=pltpu.HBM)
ANY = pl.BlockSpec(memory_space=pl.ANY)


def dot(left, right, dims=NN):
    return lax.dot_general(left, right, dims, preferred_element_type=jnp.float32)


def rotated(block, distance):
    count = lax.axis_size(AXES)
    return lax.ppermute(block, AXES, [(i, (i + distance) % count) for i in range(count)])


def swapped(block, move):
    flips = dict.fromkeys(AXES, 0)
    for axis, step in move:
        flips[axis] ^= step
    sizes = [lax.axis_size(axis) for axis in AXES]
    route = []
    for i in range(sizes[0] * sizes[1]):
        high, low = divmod(i, sizes[1])
        route.append((i, (high ^ flips[AXES[0]]) * sizes[1] + (low ^ flips[AXES[1]])))
    return lax.ppermute(block, AXES, route)


def exchange_rounds():
    bits = {axis: [1 << bit for bit in range(lax.axis_size(axis).bit_length() - 1)] for axis in AXES}
    first, rest = bits[AXES[0]][:1], bits[AXES[0]][1:]
    low, high = bits[AXES[1]][:1], bits[AXES[1]][1:]
    order = [(AXES[0], first), (AXES[1], high), (AXES[0], rest), (AXES[1], low)]
    return [(axis, step) for axis, steps in order for step in steps]


def span(index, size):
    return pl.ds(pl.multiple_of(index * size, size), size)


def sink_kernel(
    window_ref, live_ref, device_ref, key_ref, value_ref, query_ref, grad_ref, out_ref, lse_in, sink_key_ref, sink_value_ref,
    table_ref, turned_ref, row_ref, dquery_ref, sink_grad_ref, own_ref,
    *, heads, width, scale,
):
    rows = query_ref.shape[0]
    sinks = sink_key_ref.shape[0]
    sink_grad_ref[...] = jnp.zeros_like(sink_grad_ref)
    for head in range(heads):
        table_ref[head] = window_ref[head]
    table_ref[heads] = device_ref[0]
    own_ref[:, :width] = key_ref[...]
    own_ref[:, width:] = value_ref[...]
    row_ref[:heads, :] = lse_in[...] * LOG2E
    key, value = sink_key_ref[...], sink_value_ref[...]
    key_t = key.T

    at = lax.broadcasted_iota(jnp.int32, (sinks, rows), 0)

    def some_heads(step, carry):
        heads_here = [UNROLL * step + part for part in range(UNROLL)]
        query_t, grad_t, keep, delta = [], [], [], []
        for head in heads_here:
            strip = span(head, width)
            query_t.append(query_ref[:, strip].T)
            grad_t.append(grad_ref[:, strip].T)
            turned_ref[strip, :] = query_t[-1]
            turned_ref[span(heads + head, width), :] = grad_t[-1]
            product = grad_t[-1].astype(jnp.float32) * out_ref[:, strip].T.astype(jnp.float32)
            delta.append(jnp.sum(product, axis=0, keepdims=True))
            row_ref[pl.ds(heads + head, 1), :] = delta[-1]
            keep.append(at < live_ref[head])
        lse = jnp.concatenate([lse_in[pl.ds(head, 1), :] for head in heads_here], axis=1) * LOG2E
        query_t, grad_t, keep, delta = (jnp.concatenate(x, axis=1) for x in (query_t, grad_t, keep, delta))
        probs = jnp.exp2(dot(key, query_t) * (scale * LOG2E) - lse)
        probs = jnp.where(keep, probs, 0.0)
        dscores = (probs * (dot(value, grad_t) - delta)).astype(LOW)
        sink_grad_ref[:width, :] += dot(query_t, dscores, NT) * scale
        sink_grad_ref[width:, :] += dot(grad_t, probs.astype(LOW), NT)
        dquery = dot(key_t, dscores)
        for part, head in enumerate(heads_here):
            dquery_ref[span(head, width), :] = dquery[:, part * rows : (part + 1) * rows]
        return carry

    lax.fori_loop(0, heads // UNROLL, some_heads, 0)


def sum_of(refs):
    total = refs[0][...].astype(jnp.float32)
    for ref in refs[1:]:
        total = total + ref[...].astype(jnp.float32)
    return total


def mark_kernel(block_ref, same_ref):
    pass


def fold_kernel(table_ref, first_ref, second_ref, other_ref, after_ref, *refs, near):
    first_out, second_out, sum_ref = refs[-3:]
    rows = first_ref.shape[1]
    first_out[...] = (first_ref[...] + other_ref[:, :rows].astype(jnp.float32)).astype(LOW)
    other = other_ref[:, rows:].astype(jnp.float32)
    if not near:
        odd = jnp.full(other.shape, table_ref[table_ref.shape[0] - 1] & 1, jnp.int32) == 1
        other = jnp.where(odd, other, 0.0)
    second_out[...] = (second_ref[...] + other).astype(LOW)
    sum_ref[...] = sum_of(refs[:-3]).astype(sum_ref.dtype)


def near_kernel(two_ref, four_ref, *refs):
    near_ref, sum_ref = refs[-2:]
    rows = two_ref.shape[0]
    near_ref[:rows, :] = two_ref[...]
    near_ref[rows:, :] = four_ref[...]
    sum_ref[...] = sum_of(refs[:-2])


def far_kernel(table_ref, own_ref, six_ref, eight_ref, after_ref, *refs):
    far_ref, sum_ref = refs[-2:]
    rows = own_ref.shape[0]
    odd = jnp.full(own_ref.shape, table_ref[table_ref.shape[0] - 1] & 1, jnp.int32) == 1
    far_ref[:rows, :] = six_ref[...]
    far_ref[rows:, :] = jnp.where(odd, eight_ref[...], own_ref[...])
    sum_ref[...] = sum_of(refs[:-2])


def local(distances, device):
    return [
        jnp.where(device & 1 == 1, distance[1], distance[0]) if isinstance(distance, tuple) else distance
        for distance in distances
    ]


def block_kernel(*refs, layout, groups, heads, width, scale):
    refs = list(refs)

    def take(count):
        taken = refs[:count]
        del refs[:count]
        return taken

    pairs, joined, last = layout
    table_ref, turned_ref, row_ref = take(3)
    device = table_ref[heads]
    distances = local([distance for pair in pairs for distance in pair], device)
    pair_refs = take(len(pairs))
    part_refs = take(1 + len(groups)) if last else []
    other_refs = take(1) if last else []
    take(1)
    dquery_ref = take(1)[0]
    out_refs = take(1 if joined else len(distances))
    items_ref, pair_ref, key_t_ref, sum_ref = take(4)
    low_refs = take(2 * AHEAD + 4)
    total_ref, total_sems = take(2) if last else (None, None)
    rows = pair_ref.shape[1]
    unroll = 2 * UNROLL

    slot = 0
    for ref, members in zip(pair_refs, pairs):
        for place in range(len(members)):
            block = ref[place * rows : (place + 1) * rows, :]
            pair_ref[slot] = block
            key_t_ref[slot] = block[:, :width].T
            slot += 1
    sum_ref[...] = jnp.zeros_like(sum_ref)
    for ref in low_refs[4:]:
        ref[...] = jnp.zeros_like(ref)

    def needed(head, distance):
        return (table_ref[head] - distance * rows > 1 - rows) & (device >= distance)

    def list_head(head, found):
        before = found
        for slot, distance in enumerate(distances):
            items_ref[0, found] = slot
            items_ref[1, found] = head
            items_ref[2, found] = table_ref[head] - distance * rows
            items_ref[3, found] = (found == before).astype(jnp.int32)
            found = found + needed(head, distance).astype(jnp.int32)
        return found

    found = lax.fori_loop(0, heads, list_head, 0, unroll=UNROLL)
    padded = lax.div(found + UNROLL - 1, UNROLL) * UNROLL
    steps = lax.div(padded, unroll)

    def pad_item(index, carry):
        items_ref[0, index] = 0
        items_ref[1, index] = 0
        items_ref[2, index] = -rows
        items_ref[3, index] = 0
        return carry

    lax.fori_loop(found, padded, pad_item, 0)

    def produce(index, probs_ref, dscores_ref):
        slot, head, left = items_ref[0, index], items_ref[1, index], items_ref[2, index]
        strip = span(head, width)
        scores = dot(pair_ref[slot, :, :width], turned_ref[strip, :])
        probs = jnp.exp2(scores * (scale * LOG2E) - row_ref[pl.ds(head, 1), :])
        key_at = lax.broadcasted_iota(jnp.int32, (rows, 1), 0)
        query_at = lax.broadcasted_iota(jnp.int32, (1, rows), 1)
        keep = query_at - left < key_at
        if last:
            keep = keep & (key_at <= query_at)
        probs = jnp.where(keep, probs, 0.0)
        dprobs = dot(pair_ref[slot, :, width:], turned_ref[span(heads + head, width), :])
        probs_ref[...] = probs.astype(LOW)
        dscores_ref[...] = (probs * (dprobs - row_ref[pl.ds(heads + head, 1), :])).astype(LOW)

    def consume(index, probs_ref, dscores_ref):
        slot, head = items_ref[0, index], items_ref[1, index]
        strip = span(head, width)
        dscores = dscores_ref[...]
        sum_ref[slot, width:, :] += dot(turned_ref[span(heads + head, width), :], probs_ref[...], NT)
        sum_ref[slot, :width, :] += dot(turned_ref[strip, :], dscores, NT)
        dquery = dot(key_t_ref[slot], dscores)
        if last:
            dquery = dquery + part_refs[0][strip, :]
            for ref, group in zip(part_refs[1:], groups):
                touched = functools.reduce(jnp.logical_or, [needed(head, distance) for distance in local(group, device)])
                dquery = dquery + jnp.where(touched, ref[strip, :], 0.0)
            total_ref[:, strip] = dquery.T * scale
        else:
            dquery_ref[strip, :] = dquery + jnp.where(items_ref[3, index] == 1, 0.0, dquery_ref[strip, :])

    buffers = [low_refs[2 * at : 2 * at + 2] for at in range(AHEAD + 2)]

    def total_copy(step):
        lanes = span(step, UNROLL * width)
        return pltpu.make_async_copy(total_ref.at[:, lanes], dquery_ref.at[:, lanes], total_sems.at[step])

    def some_items(step, carry, count=unroll):
        for part in range(count):
            index = step * unroll + part
            produce(index, *buffers[part % len(buffers)])
            consume(jnp.maximum(index - AHEAD, 0), *buffers[(part - AHEAD) % len(buffers)])
        if last:
            total_copy(2 * step).start()
            pl.when(step > 0)(lambda: total_copy(2 * step - 1).start())
        return carry

    lax.fori_loop(0, steps, some_items, 0)
    if not last:

        @pl.when(padded > steps * unroll)
        def _():
            some_items(steps, 0, UNROLL)

    @pl.when(found > 0)
    def _():
        for at in range(UNROLL - AHEAD, UNROLL):
            consume(padded - UNROLL + at, *buffers[at % len(buffers)])

    if last:
        total_copy(heads // UNROLL - 1).start()
    for slot in range(len(distances)):
        grads = (sum_ref[slot, :width, :] * scale, sum_ref[slot, width:, :])
        for half, grad in enumerate(grads):
            strip = slice(half * width, (half + 1) * width)
            for ref in other_refs:
                other = ref[strip, rows:].astype(jnp.float32)
                grad = grad + jnp.where(jnp.full(other.shape, device & 1, jnp.int32) == 1, 0.0, other)
            if joined:
                out_refs[0][strip, slot * rows : (slot + 1) * rows] = grad.astype(out_refs[0].dtype)
            else:
                out_refs[slot][strip, :] = grad.astype(out_refs[slot].dtype)
    if last:
        for step in range(heads // UNROLL):
            total_copy(step).wait()


def block_call(pairs, pair_arrays, shared, after, parts=(), others=(), groups=(), last=False, kind=LOW, joined=False):
    table, turned, row_terms = shared
    wide, rows = turned.shape[0] // 2, turned.shape[1]
    heads = row_terms.shape[0] // 2
    width = wide // heads
    distances = [distance for pair in pairs for distance in pair]
    count = len(distances)
    shape = jax.ShapeDtypeStruct
    outs = [shape((rows, wide) if last else (wide, rows), jnp.float32)]
    outs += [shape((2 * width, count * rows), kind)] if joined else [shape((2 * width, rows), kind)] * count
    arrays = [turned, row_terms, *pair_arrays, *parts, *others, after]
    layout = (pairs, joined, last)
    return pl.pallas_call(
        functools.partial(
            block_kernel, layout=layout, groups=groups, heads=heads, width=width, scale=width**-0.5
        ),
        out_shape=outs,
        in_specs=[SMEM] + [VMEM] * (len(arrays) - 1) + [ANY],
        out_specs=[HBM if last else VMEM] + [VMEM] * (len(outs) - 1),
        scratch_shapes=[
            pltpu.SMEM((4, count * heads + 2 * UNROLL), jnp.int32),
            pltpu.VMEM((count, rows, 2 * width), LOW),
            pltpu.VMEM((count, width, rows), LOW),
            pltpu.VMEM((count, 2 * width, rows), jnp.float32),
        ]
        + [pltpu.VMEM((rows, rows), LOW)] * (2 * AHEAD + 4)
        + ([pltpu.VMEM((rows, wide), jnp.float32), pltpu.SemaphoreType.DMA((heads // UNROLL,))] if last else []),
        compiler_params=pltpu.CompilerParams(vmem_limit_bytes=VMEM_BYTES),
        cost_estimate=pl.CostEstimate(
            flops=10 * count * rows * rows * wide, bytes_accessed=2 * rows * wide, transcendentals=0
        ),
        name="blocks_" + "_".join(str(d[0] if isinstance(d, tuple) else d) for d in distances),
    )(table, *arrays)


def join_kernel(*refs, width):
    key_ref, value_ref, sink_key_ref, sink_value_ref = refs[-4:]
    turned = sum_of(refs[:5]).T
    key_ref[...] = turned[:, :width]
    value_ref[...] = turned[:, width:]
    turned = sum_of(refs[5:-4]).T
    sink_key_ref[...] = turned[:, :width]
    sink_value_ref[...] = turned[:, width:]


def on_device(
    queries, keys, values, outputs, out_grad, lse, sink_keys, sink_values, window_len, sink_live
):
    rows = queries.shape[0]
    heads = lse.shape[0]
    width = keys.shape[1]
    sinks = sink_keys.shape[0]
    wide = heads * width
    shape = jax.ShapeDtypeStruct
    device = lax.axis_index(AXES).astype(jnp.int32).reshape(1)
    own_pair = jnp.concatenate([keys, values], axis=1)
    own_pair = pl.pallas_call(
        mark_kernel,
        out_shape=shape(own_pair.shape, LOW),
        in_specs=[ANY],
        out_specs=ANY,
        input_output_aliases={0: 0},
        compiler_params=pltpu.CompilerParams(vmem_limit_bytes=1024 * 1024),
        cost_estimate=pl.CostEstimate(flops=2 * 10**10, bytes_accessed=1, transcendentals=0),
        name="mark",
    )(own_pair)
    even = {d: rotated(own_pair, d) for d in (4, 2)}

    table, turned, row_terms, dquery, sink_grad, own_held = pl.pallas_call(
        functools.partial(sink_kernel, heads=heads, width=width, scale=width**-0.5),
        out_shape=(
            shape((heads + 1,), jnp.int32),
            shape((2 * wide, rows), LOW),
            shape((2 * heads, rows), jnp.float32),
            shape((wide, rows), jnp.float32),
            shape((2 * width, sinks), jnp.float32),
            shape((rows, 2 * width), LOW),
        ),
        in_specs=[SMEM] * 3 + [VMEM] * 8,
        out_specs=(SMEM,) + (VMEM,) * 5,
        compiler_params=pltpu.CompilerParams(vmem_limit_bytes=VMEM_BYTES),
        cost_estimate=pl.CostEstimate(flops=10**10, bytes_accessed=10**6, transcendentals=0),
        name="sink_keys_part",
    )(window_len, sink_live, device, keys, values, queries, out_grad, outputs, lse, sink_keys, sink_values)

    even.update({d: rotated(own_held, d) for d in (8, 6)})
    rounds = exchange_rounds()

    def sink_terms():
        return [sink_grad] + ([swapped(sink_grad, (rounds.pop(0),))] if rounds else [])

    terms = sink_terms()
    near, sink_grad = pl.pallas_call(
        near_kernel,
        out_shape=(shape((2 * rows, 2 * width), LOW), shape(sink_grad.shape, jnp.float32)),
        in_specs=[VMEM] * (2 + len(terms)),
        out_specs=(VMEM,) * 2,
        compiler_params=pltpu.CompilerParams(vmem_limit_bytes=VMEM_BYTES),
        name="near_blocks",
    )(even[2], even[4], *terms)
    partner = ((AXES[-1], 1),)
    near_odd = swapped(near, partner)
    while len(rounds) > 4:
        sink_grad = sum(sink_terms())
    terms = sink_terms()

    shared = (table, turned, row_terms)
    parts = [dquery]
    full = jnp.float32
    near_pair, far_pair = ((1, 3), (3, 5)), ((5, 7), (7, 1))
    part, grad_2, grad_4 = block_call([(2,), (4,)], [even[2], even[4]], shared, near, kind=full)
    parts.append(part)

    far, sink_grad = pl.pallas_call(
        far_kernel,
        out_shape=(shape((2 * rows, 2 * width), LOW), shape(sink_grad.shape, jnp.float32)),
        in_specs=[SMEM] + [VMEM] * 3 + [ANY] + [VMEM] * len(terms),
        out_specs=(VMEM,) * 2,
        compiler_params=pltpu.CompilerParams(vmem_limit_bytes=VMEM_BYTES),
        name="far_blocks",
    )(table, own_held, even[6], even[8], part, *terms)
    terms = sink_terms()
    far_odd = swapped(far, partner)

    part, near_mine = block_call([near_pair], [near_odd], shared, far, joined=True)
    parts.append(part)
    near_other = swapped(near_mine, partner)

    part, far_mine = block_call([far_pair], [far_odd], shared, part, joined=True)
    parts.append(part)
    far_other = swapped(far_mine, partner)

    def fold(first, second, other, after, near):
        return pl.pallas_call(
            functools.partial(fold_kernel, near=near),
            out_shape=(shape(first.shape, LOW),) * 2 + (shape(sink_grad.shape, LOW),),
            in_specs=[SMEM] + [VMEM] * 3 + [ANY] + [VMEM] * len(terms),
            out_specs=(VMEM,) * 3,
            compiler_params=pltpu.CompilerParams(vmem_limit_bytes=VMEM_BYTES),
            name="fold",
        )(table, first, second, other, after, *terms)

    grad_2, grad_4, sink_grad = fold(grad_2, grad_4, near_other, far_mine, True)
    terms = sink_terms()
    backs = [rotated(grad_2, -2), rotated(grad_4, -4)]
    part, grad_6, grad_8 = block_call([(6,), (8,)], [even[6], even[8]], shared, grad_4, kind=full)
    parts.append(part)
    grad_6, grad_8, sink_grad = fold(grad_6, grad_8, far_other, part, False)
    terms = sink_terms()
    backs += [rotated(grad_6, -6), rotated(grad_8, -8)]
    dquery, own_grad = block_call(
        [(0,)], [own_held], shared, grad_8, parts=parts, others=(far_other,), kind=full, last=True,
        groups=((2, 4), near_pair, far_pair, (6, 8)),
    )
    key_grad, value_grad, sink_key_grad, sink_value_grad = pl.pallas_call(
        functools.partial(join_kernel, width=width),
        out_shape=(shape((rows, width), jnp.float32),) * 2 + (shape((sinks, width), jnp.float32),) * 2,
        in_specs=[VMEM] * (5 + len(terms)),
        out_specs=(VMEM,) * 4,
        compiler_params=pltpu.CompilerParams(vmem_limit_bytes=VMEM_BYTES),
        name="join",
    )(own_grad, *backs, *terms)
    return (dquery, key_grad, value_grad, sink_key_grad, sink_value_grad)


def solution(mesh):
    split = P(AXES, None)
    return jax.shard_map(
        on_device,
        mesh=mesh,
        in_specs=(split,) * 5 + (P(None, AXES),) + (P(),) * 4,
        out_specs=(split,) * 3 + (P(),) * 2,
        check_vma=False,
    )
```

```python
import functools
import math

import jax
import jax.numpy as jnp
from jax import lax
from jax.experimental import pallas as pl
from jax.experimental.pallas import tpu as pltpu
from jax.sharding import PartitionSpec as P

WIN = 2048
AXES = ("seqhi", "seqlo")
LOG2E = math.log2(math.e)
NN = (((1,), (0,)), ((), ()))
NT = (((1,), (1,)), ((), ()))
VMEM_BYTES = 22 * 1024 * 1024
UNROLL = 4
AHEAD = 2
LOW = jnp.bfloat16
VMEM = pl.BlockSpec(memory_space=pltpu.VMEM)
SMEM = pl.BlockSpec(memory_space=pltpu.SMEM)
HBM = pl.BlockSpec(memory_space=pltpu.HBM)
ANY = pl.BlockSpec(memory_space=pl.ANY)


def dot(left, right, dims=NN):
    return lax.dot_general(left, right, dims, preferred_element_type=jnp.float32)


def rotated(block, distance):
    count = lax.axis_size(AXES)
    return lax.ppermute(block, AXES, [(i, (i + distance) % count) for i in range(count)])


def swapped(block, move):
    flips = dict.fromkeys(AXES, 0)
    for axis, step in move:
        flips[axis] ^= step
    sizes = [lax.axis_size(axis) for axis in AXES]
    route = []
    for i in range(sizes[0] * sizes[1]):
        high, low = divmod(i, sizes[1])
        route.append((i, (high ^ flips[AXES[0]]) * sizes[1] + (low ^ flips[AXES[1]])))
    return lax.ppermute(block, AXES, route)


def exchange_rounds():
    bits = {axis: [1 << bit for bit in range(lax.axis_size(axis).bit_length() - 1)] for axis in AXES}
    first, rest = bits[AXES[0]][:1], bits[AXES[0]][1:]
    low, high = bits[AXES[1]][:1], bits[AXES[1]][1:]
    order = [(AXES[0], first), (AXES[1], high), (AXES[0], rest), (AXES[1], low)]
    return [(axis, step) for axis, steps in order for step in steps]


def span(index, size):
    return pl.ds(pl.multiple_of(index * size, size), size)


def sink_kernel(
    window_ref, live_ref, device_ref, key_ref, value_ref, query_ref, grad_ref, out_ref, lse_in, sink_key_ref, sink_value_ref,
    table_ref, turned_ref, row_ref, dquery_ref, sink_grad_ref, own_ref,
    *, heads, width, scale,
):
    rows = query_ref.shape[0]
    sinks = sink_key_ref.shape[0]
    sink_grad_ref[...] = jnp.zeros_like(sink_grad_ref)
    for head in range(heads):
        table_ref[head] = window_ref[head]
    table_ref[heads] = device_ref[0]
    own_ref[:, :width] = key_ref[...]
    own_ref[:, width:] = value_ref[...]
    row_ref[:heads, :] = lse_in[...] * LOG2E
    key, value = sink_key_ref[...], sink_value_ref[...]
    key_t = key.T

    at = lax.broadcasted_iota(jnp.int32, (sinks, rows), 0)

    group = 2 * UNROLL

    def some_heads(step, carry):
        heads_here = [group * step + part for part in range(group)]
        query_t, grad_t, keep, delta = [], [], [], []
        for head in heads_here:
            strip = span(head, width)
            query_t.append(query_ref[:, strip].T)
            grad_t.append(grad_ref[:, strip].T)
            turned_ref[strip, :] = query_t[-1]
            turned_ref[span(heads + head, width), :] = grad_t[-1]
            product = grad_t[-1].astype(jnp.float32) * out_ref[:, strip].T.astype(jnp.float32)
            delta.append(jnp.sum(product, axis=0, keepdims=True))
            row_ref[pl.ds(heads + head, 1), :] = delta[-1]
            keep.append(at < live_ref[head])
        lse = jnp.concatenate([lse_in[pl.ds(head, 1), :] for head in heads_here], axis=1) * LOG2E
        query_t, grad_t, keep, delta = (jnp.concatenate(x, axis=1) for x in (query_t, grad_t, keep, delta))
        probs = jnp.exp2(dot(key, query_t) * (scale * LOG2E) - lse)
        probs = jnp.where(keep, probs, 0.0)
        dscores = (probs * (dot(value, grad_t) - delta)).astype(LOW)
        sink_grad_ref[:width, :] += dot(query_t, dscores, NT) * scale
        sink_grad_ref[width:, :] += dot(grad_t, probs.astype(LOW), NT)
        dquery = dot(key_t, dscores)
        for part, head in enumerate(heads_here):
            dquery_ref[span(head, width), :] = dquery[:, part * rows : (part + 1) * rows]
        return carry

    lax.fori_loop(0, heads // group, some_heads, 0)


def sum_of(refs):
    total = refs[0][...].astype(jnp.float32)
    for ref in refs[1:]:
        total = total + ref[...].astype(jnp.float32)
    return total


def mark_kernel(block_ref, same_ref):
    pass


def fold_kernel(table_ref, first_ref, second_ref, other_ref, after_ref, *refs, near):
    first_out, second_out, sum_ref = refs[-3:]
    rows = first_ref.shape[1]
    first_out[...] = (first_ref[...] + other_ref[:, :rows].astype(jnp.float32)).astype(LOW)
    other = other_ref[:, rows:].astype(jnp.float32)
    if not near:
        odd = jnp.full(other.shape, table_ref[table_ref.shape[0] - 1] & 1, jnp.int32) == 1
        other = jnp.where(odd, other, 0.0)
    second_out[...] = (second_ref[...] + other).astype(LOW)
    sum_ref[...] = sum_of(refs[:-3]).astype(sum_ref.dtype)


def near_kernel(two_ref, four_ref, *refs):
    near_ref, sum_ref = refs[-2:]
    rows = two_ref.shape[0]
    near_ref[:rows, :] = two_ref[...]
    near_ref[rows:, :] = four_ref[...]
    sum_ref[...] = sum_of(refs[:-2])


def far_kernel(table_ref, own_ref, six_ref, eight_ref, after_ref, *refs):
    far_ref, sum_ref = refs[-2:]
    rows = own_ref.shape[0]
    odd = jnp.full(own_ref.shape, table_ref[table_ref.shape[0] - 1] & 1, jnp.int32) == 1
    far_ref[:rows, :] = six_ref[...]
    far_ref[rows:, :] = jnp.where(odd, eight_ref[...], own_ref[...])
    sum_ref[...] = sum_of(refs[:-2])


def local(distances, device):
    return [
        jnp.where(device & 1 == 1, distance[1], distance[0]) if isinstance(distance, tuple) else distance
        for distance in distances
    ]


def block_kernel(*refs, layout, groups, heads, width, scale):
    refs = list(refs)

    def take(count):
        taken = refs[:count]
        del refs[:count]
        return taken

    pairs, joined, last = layout
    table_ref, turned_ref, row_ref = take(3)
    device = table_ref[heads]
    distances = local([distance for pair in pairs for distance in pair], device)
    pair_refs = take(len(pairs))
    part_refs = take(1 + len(groups)) if last else []
    other_refs = take(1) if last else []
    take(1)
    dquery_ref = take(1)[0]
    out_refs = take(1 if joined else len(distances))
    items_ref, pair_ref, key_t_ref, sum_ref = take(4)
    low_refs = take(2 * AHEAD + 4)
    total_ref, total_sems = take(2) if last else (None, None)
    rows = pair_ref.shape[1]
    unroll = 2 * UNROLL

    slot = 0
    for ref, members in zip(pair_refs, pairs):
        for place in range(len(members)):
            block = ref[place * rows : (place + 1) * rows, :]
            pair_ref[slot] = block
            key_t_ref[slot] = block[:, :width].T
            slot += 1
    sum_ref[...] = jnp.zeros_like(sum_ref)
    for ref in low_refs[4:]:
        ref[...] = jnp.zeros_like(ref)

    def needed(head, distance):
        return (table_ref[head] - distance * rows > 1 - rows) & (device >= distance)

    def list_head(head, found):
        before = found
        for slot, distance in enumerate(distances):
            items_ref[0, found] = slot
            items_ref[1, found] = head
            items_ref[2, found] = table_ref[head] - distance * rows
            items_ref[3, found] = (found == before).astype(jnp.int32)
            found = found + needed(head, distance).astype(jnp.int32)
        return found

    found = lax.fori_loop(0, heads, list_head, 0, unroll=UNROLL)
    padded = lax.div(found + UNROLL - 1, UNROLL) * UNROLL
    steps = lax.div(padded, unroll)

    def pad_item(index, carry):
        items_ref[0, index] = 0
        items_ref[1, index] = 0
        items_ref[2, index] = -rows
        items_ref[3, index] = 0
        return carry

    lax.fori_loop(found, padded, pad_item, 0)

    def produce(index, probs_ref, dscores_ref):
        slot, head, left = items_ref[0, index], items_ref[1, index], items_ref[2, index]
        strip = span(head, width)
        scores = dot(pair_ref[slot, :, :width], turned_ref[strip, :])
        probs = jnp.exp2(scores * (scale * LOG2E) - row_ref[pl.ds(head, 1), :])
        key_at = lax.broadcasted_iota(jnp.int32, (rows, 1), 0)
        query_at = lax.broadcasted_iota(jnp.int32, (1, rows), 1)
        keep = query_at - left < key_at
        if last:
            keep = keep & (key_at <= query_at)
        probs = jnp.where(keep, probs, 0.0)
        dprobs = dot(pair_ref[slot, :, width:], turned_ref[span(heads + head, width), :])
        probs_ref[...] = probs.astype(LOW)
        dscores_ref[...] = (probs * (dprobs - row_ref[pl.ds(heads + head, 1), :])).astype(LOW)

    def consume(index, probs_ref, dscores_ref):
        slot, head = items_ref[0, index], items_ref[1, index]
        strip = span(head, width)
        dscores = dscores_ref[...]
        sum_ref[slot, width:, :] += dot(turned_ref[span(heads + head, width), :], probs_ref[...], NT)
        sum_ref[slot, :width, :] += dot(turned_ref[strip, :], dscores, NT)
        dquery = dot(key_t_ref[slot], dscores)
        if last:
            dquery = dquery + part_refs[0][strip, :]
            for ref, group in zip(part_refs[1:], groups):
                touched = functools.reduce(jnp.logical_or, [needed(head, distance) for distance in local(group, device)])
                dquery = dquery + jnp.where(touched, ref[strip, :], 0.0)
            total_ref[:, strip] = dquery.T * scale
        else:
            dquery_ref[strip, :] = dquery + jnp.where(items_ref[3, index] == 1, 0.0, dquery_ref[strip, :])

    buffers = [low_refs[2 * at : 2 * at + 2] for at in range(AHEAD + 2)]

    def total_copy(step):
        lanes = span(step, UNROLL * width)
        return pltpu.make_async_copy(total_ref.at[:, lanes], dquery_ref.at[:, lanes], total_sems.at[step])

    def some_items(step, carry, count=unroll):
        for part in range(count):
            index = step * unroll + part
            produce(index, *buffers[part % len(buffers)])
            consume(jnp.maximum(index - AHEAD, 0), *buffers[(part - AHEAD) % len(buffers)])
        if last:
            total_copy(2 * step).start()
            pl.when(step > 0)(lambda: total_copy(2 * step - 1).start())
        return carry

    lax.fori_loop(0, steps, some_items, 0)
    if not last:

        @pl.when(padded > steps * unroll)
        def _():
            some_items(steps, 0, UNROLL)

    @pl.when(found > 0)
    def _():
        for at in range(UNROLL - AHEAD, UNROLL):
            consume(padded - UNROLL + at, *buffers[at % len(buffers)])

    if last:
        total_copy(heads // UNROLL - 1).start()
    for slot in range(len(distances)):
        grads = (sum_ref[slot, :width, :] * scale, sum_ref[slot, width:, :])
        for half, grad in enumerate(grads):
            strip = slice(half * width, (half + 1) * width)
            for ref in other_refs:
                other = ref[strip, rows:].astype(jnp.float32)
                grad = grad + jnp.where(jnp.full(other.shape, device & 1, jnp.int32) == 1, 0.0, other)
            if joined:
                out_refs[0][strip, slot * rows : (slot + 1) * rows] = grad.astype(out_refs[0].dtype)
            else:
                out_refs[slot][strip, :] = grad.astype(out_refs[slot].dtype)
    if last:
        for step in range(heads // UNROLL):
            total_copy(step).wait()


def block_call(pairs, pair_arrays, shared, after, parts=(), others=(), groups=(), last=False, kind=LOW, joined=False):
    table, turned, row_terms = shared
    wide, rows = turned.shape[0] // 2, turned.shape[1]
    heads = row_terms.shape[0] // 2
    width = wide // heads
    distances = [distance for pair in pairs for distance in pair]
    count = len(distances)
    shape = jax.ShapeDtypeStruct
    outs = [shape((rows, wide) if last else (wide, rows), jnp.float32)]
    outs += [shape((2 * width, count * rows), kind)] if joined else [shape((2 * width, rows), kind)] * count
    arrays = [turned, row_terms, *pair_arrays, *parts, *others, after]
    layout = (pairs, joined, last)
    return pl.pallas_call(
        functools.partial(
            block_kernel, layout=layout, groups=groups, heads=heads, width=width, scale=width**-0.5
        ),
        out_shape=outs,
        in_specs=[SMEM] + [VMEM] * (len(arrays) - 1) + [ANY],
        out_specs=[HBM if last else VMEM] + [VMEM] * (len(outs) - 1),
        scratch_shapes=[
            pltpu.SMEM((4, count * heads + 2 * UNROLL), jnp.int32),
            pltpu.VMEM((count, rows, 2 * width), LOW),
            pltpu.VMEM((count, width, rows), LOW),
            pltpu.VMEM((count, 2 * width, rows), jnp.float32),
        ]
        + [pltpu.VMEM((rows, rows), LOW)] * (2 * AHEAD + 4)
        + ([pltpu.VMEM((rows, wide), jnp.float32), pltpu.SemaphoreType.DMA((heads // UNROLL,))] if last else []),
        compiler_params=pltpu.CompilerParams(vmem_limit_bytes=VMEM_BYTES),
        cost_estimate=pl.CostEstimate(
            flops=10 * count * rows * rows * wide, bytes_accessed=2 * rows * wide, transcendentals=0
        ),
        name="blocks_" + "_".join(str(d[0] if isinstance(d, tuple) else d) for d in distances),
    )(table, *arrays)


def join_kernel(*refs, width):
    key_ref, value_ref, sink_key_ref, sink_value_ref = refs[-4:]
    turned = sum_of(refs[:5]).T
    key_ref[...] = turned[:, :width]
    value_ref[...] = turned[:, width:]
    turned = sum_of(refs[5:-4]).T
    sink_key_ref[...] = turned[:, :width]
    sink_value_ref[...] = turned[:, width:]


def on_device(
    queries, keys, values, outputs, out_grad, lse, sink_keys, sink_values, window_len, sink_live
):
    rows = queries.shape[0]
    heads = lse.shape[0]
    width = keys.shape[1]
    sinks = sink_keys.shape[0]
    wide = heads * width
    shape = jax.ShapeDtypeStruct
    device = lax.axis_index(AXES).astype(jnp.int32).reshape(1)
    own_pair = jnp.concatenate([keys, values], axis=1)
    own_pair = pl.pallas_call(
        mark_kernel,
        out_shape=shape(own_pair.shape, LOW),
        in_specs=[ANY],
        out_specs=ANY,
        input_output_aliases={0: 0},
        compiler_params=pltpu.CompilerParams(vmem_limit_bytes=1024 * 1024),
        cost_estimate=pl.CostEstimate(flops=2 * 10**10, bytes_accessed=1, transcendentals=0),
        name="mark",
    )(own_pair)
    even = {d: rotated(own_pair, d) for d in (4, 2)}

    table, turned, row_terms, dquery, sink_grad, own_held = pl.pallas_call(
        functools.partial(sink_kernel, heads=heads, width=width, scale=width**-0.5),
        out_shape=(
            shape((heads + 1,), jnp.int32),
            shape((2 * wide, rows), LOW),
            shape((2 * heads, rows), jnp.float32),
            shape((wide, rows), jnp.float32),
            shape((2 * width, sinks), jnp.float32),
            shape((rows, 2 * width), LOW),
        ),
        in_specs=[SMEM] * 3 + [VMEM] * 8,
        out_specs=(SMEM,) + (VMEM,) * 5,
        compiler_params=pltpu.CompilerParams(vmem_limit_bytes=VMEM_BYTES),
        cost_estimate=pl.CostEstimate(flops=10**10, bytes_accessed=10**6, transcendentals=0),
        name="sink_keys_part",
    )(window_len, sink_live, device, keys, values, queries, out_grad, outputs, lse, sink_keys, sink_values)

    even.update({d: rotated(own_held, d) for d in (8, 6)})
    rounds = exchange_rounds()

    def sink_terms():
        return [sink_grad] + ([swapped(sink_grad, (rounds.pop(0),))] if rounds else [])

    terms = sink_terms()
    near, sink_grad = pl.pallas_call(
        near_kernel,
        out_shape=(shape((2 * rows, 2 * width), LOW), shape(sink_grad.shape, jnp.float32)),
        in_specs=[VMEM] * (2 + len(terms)),
        out_specs=(VMEM,) * 2,
        compiler_params=pltpu.CompilerParams(vmem_limit_bytes=VMEM_BYTES),
        name="near_blocks",
    )(even[2], even[4], *terms)
    partner = ((AXES[-1], 1),)
    near_odd = swapped(near, partner)
    while len(rounds) > 4:
        sink_grad = sum(sink_terms())
    terms = sink_terms()

    shared = (table, turned, row_terms)
    parts = [dquery]
    full = jnp.float32
    near_pair, far_pair = ((1, 3), (3, 5)), ((5, 7), (7, 1))
    part, grad_2, grad_4 = block_call([(2,), (4,)], [even[2], even[4]], shared, near, kind=full)
    parts.append(part)

    far, sink_grad = pl.pallas_call(
        far_kernel,
        out_shape=(shape((2 * rows, 2 * width), LOW), shape(sink_grad.shape, jnp.float32)),
        in_specs=[SMEM] + [VMEM] * 3 + [ANY] + [VMEM] * len(terms),
        out_specs=(VMEM,) * 2,
        compiler_params=pltpu.CompilerParams(vmem_limit_bytes=VMEM_BYTES),
        name="far_blocks",
    )(table, own_held, even[6], even[8], part, *terms)
    terms = sink_terms()
    far_odd = swapped(far, partner)

    part, near_mine = block_call([near_pair], [near_odd], shared, far, joined=True)
    parts.append(part)
    near_other = swapped(near_mine, partner)

    part, far_mine = block_call([far_pair], [far_odd], shared, part, joined=True)
    parts.append(part)
    far_other = swapped(far_mine, partner)

    def fold(first, second, other, after, near):
        return pl.pallas_call(
            functools.partial(fold_kernel, near=near),
            out_shape=(shape(first.shape, LOW),) * 2 + (shape(sink_grad.shape, LOW),),
            in_specs=[SMEM] + [VMEM] * 3 + [ANY] + [VMEM] * len(terms),
            out_specs=(VMEM,) * 3,
            compiler_params=pltpu.CompilerParams(vmem_limit_bytes=VMEM_BYTES),
            name="fold",
        )(table, first, second, other, after, *terms)

    grad_2, grad_4, sink_grad = fold(grad_2, grad_4, near_other, far_mine, True)
    terms = sink_terms()
    backs = [rotated(grad_2, -2), rotated(grad_4, -4)]
    part, grad_6, grad_8 = block_call([(6,), (8,)], [even[6], even[8]], shared, grad_4, kind=full)
    parts.append(part)
    grad_6, grad_8, sink_grad = fold(grad_6, grad_8, far_other, part, False)
    terms = sink_terms()
    backs += [rotated(grad_6, -6), rotated(grad_8, -8)]
    dquery, own_grad = block_call(
        [(0,)], [own_held], shared, grad_8, parts=parts, others=(far_other,), kind=full, last=True,
        groups=((2, 4), near_pair, far_pair, (6, 8)),
    )
    key_grad, value_grad, sink_key_grad, sink_value_grad = pl.pallas_call(
        functools.partial(join_kernel, width=width),
        out_shape=(shape((rows, width), jnp.float32),) * 2 + (shape((sinks, width), jnp.float32),) * 2,
        in_specs=[VMEM] * (5 + len(terms)),
        out_specs=(VMEM,) * 4,
        compiler_params=pltpu.CompilerParams(vmem_limit_bytes=VMEM_BYTES),
        name="join",
    )(own_grad, *backs, *terms)
    return (dquery, key_grad, value_grad, sink_key_grad, sink_value_grad)


def solution(mesh):
    split = P(AXES, None)
    return jax.shard_map(
        on_device,
        mesh=mesh,
        in_specs=(split,) * 5 + (P(None, AXES),) + (P(),) * 4,
        out_specs=(split,) * 3 + (P(),) * 2,
        check_vma=False,
    )
```
